256 devices in a mesh: dom: 8 (over y, x_lo), pix: 32 (over x_hi, z, core).
Axes of the slice: x: 4 (x_hi: 2, x_lo: 2; x = x_hi * 2 + x_lo), y: 4, z: 8, core: 2. Of those that a mesh axis runs over, the one named last changes fastest.
Arguments:
- images: bfloat16 [8192, 2, 32768], P('dom', None, 'pix'), may hold values from -6 to 6
- slices: bfloat16 [8, 256, 2, 32768], P('dom', None, None, 'pix'), may hold values from -6 to 6
- class_of: int32 [8192, 1], P('dom'), may hold values from 0 to 7, as said below
- pose_of: int32 [8192], P('dom'), may hold values from 0 to 255, as said below
- group_of: int32 [8192], P('dom'), may hold values from 0 to 63
- defocus: bfloat16 [8192], P('dom'), may hold values from 0.5 to 1.5
- slot_class: int32 [8], replicated, may hold values from 0 to 7, each once
Outputs:
- whitened: float32 [64, 12], replicated
- defocus_score: float32 [8192], P('dom')
The draws below stay inside these ranges and needn't reach their ends.
Inputs may be any that keep to these rules, and one draw needn't show every extreme that they name: Slot j of slices holds the projected slices of class slot_class[j]; every class stands in exactly one slot. `class_of`: among the 1024 particles of one device at most 192 have the same class; on every device one or two classes have exactly 192. `pose_of`: among one device's particles of one class, a pose is used a second time only after all 256 poses have been used.
All inputs are finite; a program needn't handle non-finite values.
Results may differ from the reference program's by a relative error of at most 0.0003.
Values may be sent and summed in bfloat16 or wider, within the bound.
No kernel may reach another device: no remote copies, remote signals or barrier semaphores. Data moves between devices by JAX's collectives and lax.ppermute only.
A program may use at most 128 MiB of HBM per device.

```python
import math
import jax
import jax.numpy as jnp
from jax import lax

BOX = 256
NPIX = 32768
POSES = 256
GROUPS = 64
ZERN = 12
PART_DEV = 1024
CLASSES = 8
PARTICLES = 8192
CAP = 192
N_DOM = 8


def shuffled_rows(keys, length):

    def one_row(row_key):
        return jax.random.permutation(row_key, length).astype(jnp.int32)
    return jax.vmap(one_row)(keys)


def draw_layout(key):
    blocks = CLASSES
    key_full, key_order, key_poses, key_mix = jax.random.split(key, 4)
    full_count = jax.random.randint(key_full, (blocks,), 1, 3, dtype=jnp.int32)
    full_count = jnp.minimum(full_count, PART_DEV // CAP).astype(jnp.int32)
    order = shuffled_rows(jax.random.split(key_order, blocks), CLASSES)
    pose_table = shuffled_rows(jax.random.split(key_poses, blocks * CLASSES), POSES).reshape(blocks, CLASSES * POSES)
    rank = jnp.arange(PART_DEV, dtype=jnp.int32)[None, :]
    full_col = full_count[:, None]
    head = full_col * CAP
    rest = CLASSES - full_col
    in_head = rank < head
    after = jnp.maximum(rank - head, 0)
    slot = jnp.where(in_head, rank // CAP, full_col + after % rest).astype(jnp.int32)
    within = jnp.where(in_head, rank % CAP, after // rest).astype(jnp.int32)
    labels = jnp.take_along_axis(order, slot, axis=1).astype(jnp.int32)
    poses = jnp.take_along_axis(pose_table, slot * POSES + within % POSES, axis=1).astype(jnp.int32)
    mixing = shuffled_rows(jax.random.split(key_mix, blocks), PART_DEV)
    labels = jnp.take_along_axis(labels, mixing, axis=1)
    poses = jnp.take_along_axis(poses, mixing, axis=1)
    return (labels.reshape(-1).astype(jnp.int32), poses.reshape(-1).astype(jnp.int32))


def draw_class_of(key, part):
    labels, poses = draw_layout(key)
    return labels[:, None]


def draw_pose_of(key, part):
    labels, poses = draw_layout(key)
    return poses


def touch_ends(array, key, smallest, top_value):
    extent = array.shape
    index_at = [jax.random.randint(jax.random.fold_in(key, axis), (), 0, extent[axis]) for axis in range(len(extent))]
    array = array.at[tuple(index_at)].set(smallest)
    longest = extent.index(max(extent))
    index_at[longest] = (index_at[longest] + 1) % extent[longest]
    return array.at[tuple(index_at)].set(top_value)


def block_scale(own_key, shape, pieces, least, largest):
    factor_of = 1.0
    for axis_at, blocks in pieces:
        draws = jax.random.uniform(jax.random.fold_in(jax.random.fold_in(own_key, 6), axis_at), (blocks,), jnp.float32, least / len(pieces), largest / len(pieces))
        factor_of = factor_of * jnp.repeat(jnp.exp(draws), shape[axis_at] // blocks).reshape((-1,) + (1,) * (len(shape) - 1 - axis_at))
    return factor_of


def gaussian(rng, dims, width, most, cuts=(), kind=jnp.bfloat16):
    level = block_scale(rng, dims, cuts, -0.22, 0.18) if cuts else 1.0
    values = jax.random.normal(rng, dims, jnp.float32) * width * level
    return jnp.minimum(jnp.maximum(values, -most), most).astype(kind)


def setup_inputs(seed: int = 0) -> dict:
    arg_keys = jax.random.split(jax.random.key(seed), 8)
    images = gaussian(arg_keys[0], (PARTICLES, 2, NPIX), 1.0, 6.0, ((0, 8), (2, 32)))
    slices = gaussian(arg_keys[1], (CLASSES, POSES, 2, NPIX), 1.0, 6.0, ((0, 8), (3, 32)))
    class_of = draw_class_of(jax.random.fold_in(arg_keys[7], 71), 0)
    pose_of = draw_pose_of(jax.random.fold_in(arg_keys[7], 71), 0)
    group_of = touch_ends(jax.random.randint(arg_keys[4], (PARTICLES,), 0, GROUPS), jax.random.fold_in(arg_keys[4], 1), 0, GROUPS - 1).astype(jnp.int32)
    defocus = jnp.clip(0.5 + 1.0 * jax.random.uniform(arg_keys[5], (PARTICLES,), jnp.float32) ** block_scale(arg_keys[5], (PARTICLES,), ((0, 8),), -0.2, 0.2), 0.5, 1.5).astype(jnp.bfloat16)
    slot_class = jax.random.permutation(arg_keys[6], CLASSES).astype(jnp.int32)
    return dict(images=images, slices=slices, class_of=class_of, pose_of=pose_of, group_of=group_of, defocus=defocus, slot_class=slot_class)


PHASE_GAIN = 40.0
RIDGE = 1.0

def pixel_grid(pix_start, pix_count):
    pixel_index = pix_start + jnp.arange(pix_count, dtype=jnp.int32)
    half_box = BOX // 2
    radial_scale = math.sqrt(2.0) / BOX
    freq_x = (pixel_index % half_box).astype(jnp.float32) * radial_scale
    freq_y = (pixel_index // half_box - half_box).astype(jnp.float32) * radial_scale
    return (freq_x, freq_y)

def zernike(freq_x, freq_y):
    radius_sq = freq_x * freq_x + freq_y * freq_y
    real_one, imag_one = (freq_x, freq_y)
    real_two = freq_x * freq_x - freq_y * freq_y
    imag_two = 2.0 * freq_x * freq_y
    real_three = real_two * real_one - imag_two * imag_one
    imag_three = real_two * imag_one + imag_two * real_one
    real_five = real_three * real_two - imag_three * imag_two
    imag_five = real_three * imag_two + imag_three * real_two
    radial_three = 3.0 * radius_sq - 2.0
    radial_five = 10.0 * radius_sq * radius_sq - 12.0 * radius_sq + 3.0
    radial_outer = 5.0 * radius_sq - 4.0
    return jnp.stack([real_one, imag_one, radial_three * real_one, radial_three * imag_one, radial_five * real_one, radial_five * imag_one, real_three, imag_three, radial_outer * real_three, radial_outer * imag_three, real_five, imag_five])

def particle_terms(row_block, projected, defocus_rows, radius_sq):
    phase_chi = PHASE_GAIN * defocus_rows.astype(jnp.float32)[:, None] * radius_sq[None, :]
    ctf_value = -jnp.sin(phase_chi)
    ctf_slope = -PHASE_GAIN * radius_sq[None, :] * jnp.cos(phase_chi)
    proj_real = projected[:, 0, :].astype(jnp.float32)
    proj_imag = projected[:, 1, :].astype(jnp.float32)
    image_real = row_block[:, 0, :].astype(jnp.float32)
    image_imag = row_block[:, 1, :].astype(jnp.float32)
    pred_real = ctf_value * proj_real
    pred_imag = ctf_value * proj_imag
    pred_power = pred_real * pred_real + pred_imag * pred_imag
    cross_term = pred_real * image_imag - pred_imag * image_real
    gradient = lax.optimization_barrier(jnp.sum(ctf_slope * (proj_real * (pred_real - image_real) + proj_imag * (pred_imag - image_imag)), axis=1))
    curvature = lax.optimization_barrier(jnp.sum(ctf_slope * ctf_slope * (proj_real * proj_real + proj_imag * proj_imag), axis=1))
    return (pred_power, cross_term, gradient, curvature)

def contract(group_sums, zernike_basis, pix_count):
    pair_table = (zernike_basis[:, None, :] * zernike_basis[None, :, :]).reshape(ZERN * ZERN, pix_count)
    power_sums = group_sums[:, :pix_count]
    cross_sums = group_sums[:, pix_count:]
    normal_flat = jnp.dot(power_sums, pair_table.T, precision=lax.Precision.HIGHEST)
    right_side = jnp.dot(cross_sums, zernike_basis.T, precision=lax.Precision.HIGHEST)
    return (normal_flat, right_side)

def whiten(normal_flat, right_side):
    normal = normal_flat.reshape(GROUPS, ZERN, ZERN) + RIDGE * jnp.eye(ZERN, dtype=jnp.float32)
    factor = jnp.linalg.cholesky(normal)
    solved = lax.linalg.triangular_solve(factor, right_side[:, :, None], left_side=True, lower=True)
    return solved[:, :, 0]

def reference(images, slices, class_of, pose_of, group_of, defocus, slot_class):
    freq_x, freq_y = pixel_grid(0, NPIX)
    radius_sq = freq_x * freq_x + freq_y * freq_y
    zernike_basis = zernike(freq_x, freq_y)
    class_col = class_of[:, 0]
    slot_ids = jnp.arange(CLASSES, dtype=jnp.int32)
    slot_of = lax.optimization_barrier(jnp.sum(jnp.where(slot_class[None, :] == class_col[:, None], slot_ids[None, :], 0), axis=1)).astype(jnp.int32)

    def one_block(group_sums, block_index):
        first_row = (block_index * PART_DEV).astype(jnp.int32)
        row_block = lax.dynamic_slice_in_dim(images, first_row, PART_DEV, 0)
        slot_block = lax.dynamic_slice_in_dim(slot_of, first_row, PART_DEV, 0)
        pose_block = lax.dynamic_slice_in_dim(pose_of, first_row, PART_DEV, 0)
        group_block = lax.dynamic_slice_in_dim(group_of, first_row, PART_DEV, 0)
        defocus_rows = lax.dynamic_slice_in_dim(defocus, first_row, PART_DEV, 0)
        projected = slices[slot_block, pose_block]
        pred_power, cross_term, gradient, curvature = particle_terms(row_block, projected, defocus_rows, radius_sq)
        joined = jnp.concatenate([pred_power, cross_term], axis=1)
        group_sums = group_sums + jax.ops.segment_sum(joined, group_block, num_segments=GROUPS)
        return (group_sums, (gradient, curvature))
    start_sums = jnp.zeros((GROUPS, 2 * NPIX), jnp.float32)
    group_sums, (gradient, curvature) = lax.scan(one_block, start_sums, jnp.arange(N_DOM, dtype=jnp.int32))
    gradient = gradient.reshape(-1)
    curvature = curvature.reshape(-1)
    defocus_score = -gradient * lax.rsqrt(curvature + 1e-06)
    normal_flat, right_side = contract(group_sums, zernike_basis, NPIX)
    whitened = whiten(normal_flat, right_side)
    return (whitened, defocus_score)
```

```python
import functools
import math

import jax
import jax.numpy as jnp
from jax import lax
from jax.experimental import pallas as pl
from jax.experimental.pallas import tpu as pltpu
from jax.sharding import PartitionSpec as P

BOX = 256
GROUPS = 64
ZERN = 12
PAIRS = ZERN * (ZERN + 1) // 2
PHASE_GAIN = 40.0
RIDGE = 1.0

CHUNKS = 4
ROWS = 256
MOMENTS = 96
RIGHT_AT = 80

SIN_POLY = (3.141592580044675, -5.167706878922935, 2.5500313772212047, -0.5980451737557255, 0.07722012821305138)
COS_POLY = (0.9999999534415752, -4.934792857330457, 4.058411894717311, -1.3318800570964462, 0.2196966127309024)

X_SWAP = [(d, d ^ 1) for d in range(8)]
Y_UP = [(d, (d + 2) % 8) for d in range(8)]
Y_DOWN = [(d, (d - 2) % 8) for d in range(8)]
CORE_SWAP = [(p, p ^ 1) for p in range(32)]
CORE_GROUPS = [[2 * m + c for m in range(16)] for c in range(2)]

F32 = jnp.float32
BF16 = jnp.bfloat16
SMEM = pl.BlockSpec(memory_space=pltpu.SMEM)
VMEM = pl.BlockSpec(memory_space=pltpu.VMEM)


def params():
    return pltpu.CompilerParams(vmem_limit_bytes=40 * 1024 * 1024)


def horner(coeffs, z):
    acc = jnp.full_like(z, coeffs[-1])
    for c in coeffs[-2::-1]:
        acc = acc * z + c
    return acc


def hot_kernel(place, slot_class, class_ref, pose_ref, hot_ref):
    y0 = place[0] >> 1
    x0 = place[0] & 1
    cls = class_ref[...]
    block = jnp.zeros_like(cls)
    for slot in range(8):
        near = ((((slot >> 1) - y0) & 3) << 1) | ((slot & 1) ^ x0)
        block = jnp.where(cls == slot_class[slot], near, block)
    row = block * 256 + pose_ref[...]
    col = lax.broadcasted_iota(jnp.int32, hot_ref.shape, 1)
    hot_ref[...] = jnp.where(col == row, 1.0, 0.0).astype(BF16)


def hot_rows(place, slot_class, class_of, pose_of):
    parts = class_of.shape[0]
    return pl.pallas_call(
        hot_kernel,
        grid=(parts // ROWS,),
        in_specs=[
            SMEM,
            SMEM,
            pl.BlockSpec((ROWS, 1), lambda i: (i, 0)),
            pl.BlockSpec((ROWS, 1), lambda i: (i, 0)),
        ],
        out_specs=pl.BlockSpec((ROWS, 2048), lambda i: (i, 0)),
        out_shape=jax.ShapeDtypeStruct((parts, 2048), BF16),
        compiler_params=params(),
        name="hot_rows",
    )(place, slot_class, class_of, pose_of)


def pixel_grid(first, count):
    index = first + lax.broadcasted_iota(jnp.int32, (1, count), 1)
    scale = math.sqrt(2.0) / BOX
    freq_x = (index & (BOX // 2 - 1)).astype(F32) * scale
    freq_y = ((index >> 7) - BOX // 2).astype(F32) * scale
    return freq_x, freq_y


def zernike_rows(freq_x, freq_y):
    q = freq_x * freq_x + freq_y * freq_y
    re1, im1 = freq_x, freq_y
    re2 = freq_x * freq_x - freq_y * freq_y
    im2 = 2.0 * freq_x * freq_y
    re3 = re2 * re1 - im2 * im1
    im3 = re2 * im1 + im2 * re1
    re5 = re3 * re2 - im3 * im2
    im5 = re3 * im2 + im3 * re2
    r3 = 3.0 * q - 2.0
    r5 = 10.0 * q * q - 12.0 * q + 3.0
    ro = 5.0 * q - 4.0
    return [re1, im1, r3 * re1, r3 * im1, r5 * re1, r5 * im1, re3, im3, ro * re3, ro * im3, re5, im5]


def chunk_kernel(fill, first, hot_ref, re_ref, im_ref, defocus_ref, group_ref, *rest):
    pieces = rest[: -6]
    moment_ref, grad_ref, table, sums, basis, pairs = rest[-6:]
    step = pl.program_id(0)
    count = re_ref.shape[1]
    freq_x, freq_y = pixel_grid(first[0], count)
    q = freq_x * freq_x + freq_y * freq_y

    @pl.when(step == 0)
    def _():
        for piece, src, dst, rows in fill:
            table[dst : dst + rows, :] = pieces[piece][src : src + rows, :]
        sums[...] = jnp.zeros_like(sums)

    proj = jnp.dot(hot_ref[...], table[...], preferred_element_type=F32)
    proj_re = proj[:, :count]
    proj_im = proj[:, count:]
    image_re = re_ref[...].astype(F32)
    image_im = im_ref[...].astype(F32)

    turns = (defocus_ref[...] * (PHASE_GAIN / (2.0 * math.pi))) * q
    rest_turn = turns - jnp.floor(turns + 0.5)
    z = rest_turn * rest_turn
    s = rest_turn * horner(SIN_POLY, z)
    c = horner(COS_POLY, z)
    s2 = s + s
    sin_phi = s2 * c
    cos_phi = 1.0 - s2 * s

    power = proj_re * proj_re + proj_im * proj_im
    along = proj_re * image_re + proj_im * image_im
    across = proj_im * image_re - proj_re * image_im
    weight = (PHASE_GAIN * q) * cos_phi
    sp = sin_phi * power
    grad = weight * (sp + along)
    curv = weight * weight * power
    pred_power = sin_phi * sp
    cross = sin_phi * across

    cross_hi = cross.astype(BF16)
    cross_lo = (cross - cross_hi.astype(F32)).astype(BF16)
    group_hot = jnp.where(
        lax.broadcasted_iota(jnp.int32, (GROUPS, ROWS), 0) == group_ref[...], 1.0, 0.0
    ).astype(BF16)
    sums[:, 0:count] += jnp.dot(group_hot, pred_power.astype(BF16), preferred_element_type=F32)
    sums[:, count:] += jnp.dot(group_hot, cross_hi, preferred_element_type=F32) + jnp.dot(
        group_hot, cross_lo, preferred_element_type=F32
    )

    def lanes(v):
        return sum(v[:, 128 * i : 128 * i + 128] for i in range(count // 128))

    grad_ref[0:1, :] = jnp.sum(lanes(grad).T, axis=0, keepdims=True)
    grad_ref[1:2, :] = jnp.sum(lanes(curv).T, axis=0, keepdims=True)

    @pl.when(step == pl.num_programs(0) - 1)
    def _():
        basis[...] = jnp.zeros_like(basis)
        for j, row in enumerate(zernike_rows(freq_x, freq_y)):
            basis[j : j + 1, :] = row
        pairs[72:80, :] = jnp.zeros((8, count), F32)
        at = 0
        for j in range(ZERN):
            pairs[at : at + ZERN - j, :] = basis[j : j + 1, :] * basis[j:ZERN, :]
            at += ZERN - j
        nt = (((1,), (1,)), ((), ()))
        moment_ref[0:RIGHT_AT, :] = lax.dot_general(
            pairs[...], sums[:, :count], nt, precision=lax.Precision.HIGHEST, preferred_element_type=F32
        )
        moment_ref[RIGHT_AT:, :] = lax.dot_general(
            basis[...], sums[:, count:], nt, precision=lax.Precision.HIGHEST, preferred_element_type=F32
        )


def chunk_terms(chunk, fill, first, hot, images, defocus_col, group_row, pieces):
    parts = hot.shape[0]
    count = images.shape[1] // (2 * CHUNKS)
    return pl.pallas_call(
        functools.partial(chunk_kernel, fill),
        grid=(parts // ROWS,),
        in_specs=[
            SMEM,
            pl.BlockSpec((ROWS, 2048), lambda i: (i, 0)),
            pl.BlockSpec((ROWS, count), lambda i: (i, chunk)),
            pl.BlockSpec((ROWS, count), lambda i: (i, CHUNKS + chunk)),
            pl.BlockSpec((ROWS, 1), lambda i: (i, 0)),
            pl.BlockSpec((1, ROWS), lambda i: (0, i)),
        ]
        + [pl.BlockSpec(p.shape, lambda i: (0, 0)) for p in pieces],
        out_specs=[
            pl.BlockSpec((MOMENTS, GROUPS), lambda i: (0, 0)),
            pl.BlockSpec((2, ROWS), lambda i: (0, i)),
        ],
        out_shape=[
            jax.ShapeDtypeStruct((MOMENTS, GROUPS), F32),
            jax.ShapeDtypeStruct((2, parts), F32),
        ],
        scratch_shapes=[
            pltpu.VMEM((2048, 2 * count), BF16),
            pltpu.VMEM((GROUPS, 2 * count), F32),
            pltpu.VMEM((16, count), F32),
            pltpu.VMEM((RIGHT_AT, count), F32),
        ],
        compiler_params=params(),
        cost_estimate=pl.CostEstimate(
            flops=2 * parts * 2048 * 2 * count, bytes_accessed=8 * 1024 * 1024, transcendentals=0
        ),
        name="chunk_terms",
    )(first, hot, images, images, defocus_col, group_row, *pieces)


def pack_kernel(core, *refs):
    keep_ref, send_ref, full = refs[-3:]
    moments = sum(r[...] for r in refs[:CHUNKS])
    grads = sum(r[...] for r in refs[CHUNKS : 2 * CHUNKS])
    half = MOMENTS // 2
    packed = jnp.concatenate([moments[:half], moments[half:]], axis=1)
    for h in range(2):
        full[32 * h : 32 * h + 24, :] = packed[24 * h : 24 * h + 24]
        for r in range(4):
            at = 512 * h + 128 * r
            full[32 * h + 24 + r : 32 * h + 25 + r, :] = grads[0:1, at : at + 128]
            full[32 * h + 28 + r : 32 * h + 29 + r, :] = grads[1:2, at : at + 128]
    keep_ref[...] = full[pl.ds(pl.multiple_of(core[0] * 32, 32), 32), :]
    send_ref[...] = full[pl.ds(pl.multiple_of((1 - core[0]) * 32, 32), 32), :]


def spread_dom_kernel(a_ref, b_ref, out_ref, grad_ref):
    total = a_ref[...] + b_ref[...]
    grad_ref[...] = total[24:]
    for i in range(8):
        out_ref[i] = total[:24]


def spread_pix_kernel(in_ref, grad_ref, out_ref):
    total = in_ref[0]
    for i in range(1, 8):
        total = total + in_ref[i]
    grad = grad_ref[...]
    for i in range(16):
        out_ref[i, 0:24] = total
        out_ref[i, 24:32] = grad


def total_kernel(in_ref, out_ref):
    total = in_ref[0]
    for i in range(1, 16):
        total = total + in_ref[i]
    out_ref[...] = total


def whiten_kernel(core, own_ref, other_ref, white_ref, score_ref, both, rows):
    both[pl.ds(pl.multiple_of(core[0] * 32, 32), 32), :] = own_ref[...]
    both[pl.ds(pl.multiple_of((1 - core[0]) * 32, 32), 32), :] = other_ref[...]
    low = jnp.concatenate([both[0:24, :], both[32:56, :]], axis=0)
    moments = jnp.concatenate([low[:, :GROUPS], low[:, GROUPS:]], axis=0)
    at = 0
    rows[...] = jnp.zeros_like(rows)
    for j in range(ZERN):
        rows[j, j:ZERN, :] = moments[at : at + ZERN - j]
        at += ZERN - j
    right = moments[RIGHT_AT : RIGHT_AT + 16]
    line = [rows[j] for j in range(ZERN)]
    lane_row = lax.broadcasted_iota(jnp.int32, (16, GROUPS), 0)
    done = jnp.zeros((16, GROUPS), F32)
    for j in range(ZERN):
        inv = lax.rsqrt(line[j][j : j + 1] + RIDGE)
        col = line[j] * inv
        value = right[j : j + 1] * inv
        done = jnp.where(lane_row == j, value, done)
        right = right - col * value
        for i in range(j + 1, ZERN):
            line[i] = line[i] - col[i : i + 1] * col
    white_ref[...] = done.T[:, :ZERN]
    for h in range(2):
        grad = both[32 * h + 24 : 32 * h + 28, :]
        curv = both[32 * h + 28 : 32 * h + 32, :]
        score_ref[4 * h : 4 * h + 4, :] = -grad * lax.rsqrt(curv + 1e-06)


def reduce_all(core, moments, grads):
    half = jax.ShapeDtypeStruct((32, 128), F32)
    keep, send = pl.pallas_call(
        pack_kernel,
        in_specs=[SMEM] + [VMEM] * (2 * CHUNKS),
        out_shape=[half, half],
        scratch_shapes=[pltpu.VMEM((64, 128), F32)],
        name="pack",
    )(core, *moments, *grads)
    other = lax.ppermute(send, "pix", CORE_SWAP)
    spread, grad = pl.pallas_call(
        spread_dom_kernel,
        out_shape=[jax.ShapeDtypeStruct((8, 24, 128), F32), jax.ShapeDtypeStruct((8, 128), F32)],
        name="spread_dom",
    )(keep, other)
    spread = lax.all_to_all(spread, "dom", 0, 0)
    spread = pl.pallas_call(
        spread_pix_kernel,
        out_shape=jax.ShapeDtypeStruct((16, 32, 128), F32),
        name="spread_pix",
    )(spread, grad)
    spread = lax.all_to_all(spread, "pix", 0, 0, axis_index_groups=CORE_GROUPS)
    own = pl.pallas_call(total_kernel, out_shape=half, name="total")(spread)
    other = lax.ppermute(own, "pix", CORE_SWAP)
    white, score = pl.pallas_call(
        whiten_kernel,
        in_specs=[SMEM, VMEM, VMEM],
        out_shape=[
            jax.ShapeDtypeStruct((GROUPS, ZERN), F32),
            jax.ShapeDtypeStruct((8, 128), F32),
        ],
        scratch_shapes=[pltpu.VMEM((64, 128), F32), pltpu.VMEM((ZERN, 16, GROUPS), F32)],
        name="whiten",
    )(core, own, other)
    return white, score.reshape(-1)


def hop(block, perm):
    return lax.ppermute(block, "dom", perm)


FILL_X_FIRST = [(0, 0, 0, 512), (1, 0, 1536, 512), (2, 0, 512, 512), (3, 0, 1024, 256), (4, 0, 1280, 256)]
FILL_Y_FIRST = [(0, 0, 0, 256), (0, 256, 1536, 256), (0, 512, 512, 256), (0, 768, 1024, 256)] + [
    (1, 0, 256, 256),
    (1, 256, 1792, 256),
    (1, 512, 768, 256),
    (1, 768, 1280, 256),
]


def gather_x_first(own):
    pair = jnp.concatenate([own, hop(own, X_SWAP)], axis=0)
    below = hop(pair, Y_UP)
    above = hop(pair, Y_DOWN)
    far_0 = hop(below[:256], Y_UP)
    far_1 = hop(above[256:], Y_DOWN)
    return [pair, below, above, far_0, far_1]


def gather_y_first(own):
    below = hop(own, Y_UP)
    above = hop(own, Y_DOWN)
    far_0 = hop(below[:128], Y_UP)
    far_1 = hop(above[128:], Y_DOWN)
    column = jnp.concatenate([own, below, above, far_0, far_1], axis=0)
    return [column, hop(column, X_SWAP)]


def local(images, slices, class_of, pose_of, group_of, defocus, slot_class):
    parts, _, pix_count = images.shape
    poses = slices.shape[1]
    count = pix_count // CHUNKS
    dom_at = lax.axis_index("dom").astype(jnp.int32).reshape(1)
    pix_at = lax.axis_index("pix").astype(jnp.int32)
    core = (pix_at & 1).reshape(1)
    flat = slices.reshape(poses, 2 * pix_count)
    own = [
        jnp.concatenate(
            [flat[:, c * count : (c + 1) * count], flat[:, pix_count + c * count : pix_count + (c + 1) * count]],
            axis=1,
        )
        for c in range(CHUNKS)
    ]
    gathered = {0: gather_y_first(own[0]), 1: gather_x_first(own[1]), 2: gather_x_first(own[2]), 3: gather_y_first(own[3])}
    hot = hot_rows(dom_at, slot_class, class_of, pose_of[:, None])
    image_rows = images.reshape(parts, 2 * pix_count)
    defocus_col = defocus.astype(F32)[:, None]
    group_row = group_of[None, :]
    moments, grads = [], []
    for c in range(CHUNKS):
        fill = FILL_Y_FIRST if c in (0, 3) else FILL_X_FIRST
        first = (pix_at * pix_count + c * count).reshape(1)
        m, g = chunk_terms(c, fill, first, hot, image_rows, defocus_col, group_row, gathered[c])
        moments.append(m)
        grads.append(g)
    return reduce_all(core, moments, grads)


def solution(mesh):
    return jax.shard_map(
        local,
        mesh=mesh,
        in_specs=(
            P("dom", None, "pix"),
            P("dom", None, None, "pix"),
            P("dom", None),
            P("dom"),
            P("dom"),
            P("dom"),
            P(),
        ),
        out_specs=(P(), P("dom")),
        check_vma=False,
    )
```

```python
import functools
import math

import jax
import jax.numpy as jnp
from jax import lax
from jax.experimental import pallas as pl
from jax.experimental.pallas import tpu as pltpu
from jax.sharding import PartitionSpec as P

BOX = 256
GROUPS = 64
ZERN = 12
PAIRS = ZERN * (ZERN + 1) // 2
PHASE_GAIN = 40.0
RIDGE = 1.0

ROWS = 512
WIDE = 256
MOMENTS = 96
RIGHT_AT = 80

SIN_POLY = (3.141592580044675, -5.167706878922935, 2.5500313772212047, -0.5980451737557255, 0.07722012821305138)
COS_POLY = (0.9999999534415752, -4.934792857330457, 4.058411894717311, -1.3318800570964462, 0.2196966127309024)

X_SWAP = [(d, d ^ 1) for d in range(8)]
Y_UP = [(d, (d + 2) % 8) for d in range(8)]
Y_DOWN = [(d, (d - 2) % 8) for d in range(8)]
CORE_SWAP = [(p, p ^ 1) for p in range(32)]
CORE_GROUPS = [[2 * m + c for m in range(16)] for c in range(2)]

F32 = jnp.float32
BF16 = jnp.bfloat16
SMEM = pl.BlockSpec(memory_space=pltpu.SMEM)
VMEM = pl.BlockSpec(memory_space=pltpu.VMEM)


def params():
    return pltpu.CompilerParams(vmem_limit_bytes=28 * 1024 * 1024)


def horner(coeffs, z):
    acc = jnp.full_like(z, coeffs[-1])
    for c in coeffs[-2::-1]:
        acc = acc * z + c
    return acc


def pixel_grid(first, count):
    index = first + lax.broadcasted_iota(jnp.int32, (1, count), 1)
    scale = math.sqrt(2.0) / BOX
    freq_x = (index & (BOX // 2 - 1)).astype(F32) * scale
    freq_y = ((index >> 7) - BOX // 2).astype(F32) * scale
    return freq_x, freq_y


def zernike_rows(freq_x, freq_y):
    q = freq_x * freq_x + freq_y * freq_y
    re1, im1 = freq_x, freq_y
    re2 = freq_x * freq_x - freq_y * freq_y
    im2 = 2.0 * freq_x * freq_y
    re3 = re2 * re1 - im2 * im1
    im3 = re2 * im1 + im2 * re1
    re5 = re3 * re2 - im3 * im2
    im5 = re3 * im2 + im3 * re2
    r3 = 3.0 * q - 2.0
    r5 = 10.0 * q * q - 12.0 * q + 3.0
    ro = 5.0 * q - 4.0
    return [re1, im1, r3 * re1, r3 * im1, r5 * re1, r5 * im1, re3, im3, ro * re3, ro * im3, re5, im5]


def chunk_kernel(spec, refs):
    fill, start, count, begins, ends = spec
    refs = list(refs)
    if ends:
        core = refs.pop(0)
    first, mark_ref, group_ref = refs[:3]
    refs = refs[3:]
    if not begins:
        old_moments, old_grads = refs[:2]
        refs = refs[2:]
    image_ref = refs.pop(0)
    refs, work = refs[:-10], refs[-10:]
    table, image, hot, sums, basis, pairs, proj_0, proj_1, table_sem, image_sem = work
    proj = [proj_0, proj_1]
    if ends:
        keep_ref, send_ref, moment_ref, grad_ref, full = refs[-5:]
        pieces = refs[:-5]
    else:
        moment_ref, grad_ref = refs[-2:]
        pieces = refs[:-2]
    parts = mark_ref.shape[0]
    pix_count = image_ref.shape[1] // 2

    loads = [
        pltpu.make_async_copy(
            pieces[piece].at[pl.ds(src, rows), :], table.at[pl.ds(dst, rows), :], table_sem.at[i]
        )
        for i, (piece, src, dst, rows) in enumerate(fill)
    ]
    image_loads = [
        pltpu.make_async_copy(
            image_ref.at[:, pl.ds(part * pix_count + start, count)],
            image.at[:, pl.ds(part * count, count)],
            image_sem.at[part],
        )
        for part in range(2)
    ]
    for copy in loads + image_loads:
        copy.start()
    sums[...] = jnp.zeros_like(sums)
    freq_x, freq_y = pixel_grid(first[0] + start, count)
    q = freq_x * freq_x + freq_y * freq_y

    def lanes(v):
        return sum(v[:, 128 * i : 128 * i + 128] for i in range(v.shape[1] // 128))

    n_blocks = (parts // ROWS) * (count // WIDE)

    def mark_hot(r):
        row = mark_ref[r * ROWS : (r + 1) * ROWS, 0:1].astype(jnp.int32)
        col = lax.broadcasted_iota(jnp.int32, (ROWS, 256), 1)
        for kb in range(8):
            hot[:, 256 * kb : 256 * kb + 256] = jnp.where(col == row - 256 * kb, 1.0, 0.0).astype(BF16)

    def pick(k):
        r, sub = divmod(k, count // WIDE)
        if sub == 0:
            mark_hot(r)
        at = sub * WIDE
        proj[k % 2][:, :WIDE] = jnp.dot(hot[...], table[:, at : at + WIDE], preferred_element_type=F32)
        proj[k % 2][:, WIDE:] = jnp.dot(
            hot[...], table[:, count + at : count + at + WIDE], preferred_element_type=F32
        )

    for copy in loads:
        copy.wait()
    pick(0)
    for copy in image_loads:
        copy.wait()

    def rows_step(r, _):
        here = slice(r * ROWS, (r + 1) * ROWS)
        defocus = mark_ref[here, 1:2] * (PHASE_GAIN / (2.0 * math.pi))
        group_hot = jnp.where(
            lax.broadcasted_iota(jnp.int32, (GROUPS, ROWS), 0) == group_ref[:, here], 1.0, 0.0
        ).astype(BF16)
        grad_sum = 0.0
        curv_sum = 0.0
        for sub in range(0, count, WIDE):
            cols = slice(sub, sub + WIDE)
            other = slice(count + sub, count + sub + WIDE)
            k = r * (count // WIDE) + sub // WIDE
            if k + 1 < n_blocks:
                pick(k + 1)
            proj_re = proj[k % 2][:, :WIDE]
            proj_im = proj[k % 2][:, WIDE:]
            image_re = image[here, sub : sub + WIDE].astype(F32)
            image_im = image[here, count + sub : count + sub + WIDE].astype(F32)
            q_sub = q[:, cols]

            turns = defocus * q_sub
            rest_turn = turns - jnp.floor(turns + 0.5)
            z = rest_turn * rest_turn
            s = rest_turn * horner(SIN_POLY, z)
            c = horner(COS_POLY, z)
            s2 = s + s
            sin_phi = s2 * c
            cos_phi = 1.0 - s2 * s

            power = proj_re * proj_re + proj_im * proj_im
            along = proj_re * image_re + proj_im * image_im
            across = proj_im * image_re - proj_re * image_im
            weight = (PHASE_GAIN * q_sub) * cos_phi
            sp = sin_phi * power
            grad_sum += lanes(weight * (sp + along))
            curv_sum += lanes(weight * weight * power)
            pred_power = sin_phi * sp
            cross = sin_phi * across

            cross_hi = cross.astype(BF16)
            cross_lo = (cross - cross_hi.astype(F32)).astype(BF16)
            sums[:, cols] += jnp.dot(group_hot, pred_power.astype(BF16), preferred_element_type=F32)
            sums[:, other] += jnp.dot(group_hot, cross_hi, preferred_element_type=F32) + jnp.dot(
                group_hot, cross_lo, preferred_element_type=F32
            )
        grad_row = jnp.sum(grad_sum.T, axis=0, keepdims=True)
        curv_row = jnp.sum(curv_sum.T, axis=0, keepdims=True)
        if not begins:
            grad_row = grad_row + old_grads[0:1, here]
            curv_row = curv_row + old_grads[1:2, here]
        grad_ref[0:1, here] = grad_row
        grad_ref[1:2, here] = curv_row
        return 0

    for r in range(parts // ROWS):
        rows_step(r, 0)

    basis[...] = jnp.zeros_like(basis)
    for j, row in enumerate(zernike_rows(freq_x, freq_y)):
        basis[j : j + 1, :] = row
    pairs[72:80, :] = jnp.zeros((8, count), F32)
    at = 0
    for j in range(ZERN):
        pairs[at : at + ZERN - j, :] = basis[j : j + 1, :] * basis[j:ZERN, :]
        at += ZERN - j
    nt = (((1,), (1,)), ((), ()))
    normal = lax.dot_general(
        pairs[...], sums[:, :count], nt, precision=lax.Precision.HIGHEST, preferred_element_type=F32
    )
    right = lax.dot_general(
        basis[...], sums[:, count:], nt, precision=lax.Precision.HIGHEST, preferred_element_type=F32
    )
    if not begins:
        normal = normal + old_moments[0:RIGHT_AT, :]
        right = right + old_moments[RIGHT_AT:, :]
    moment_ref[0:RIGHT_AT, :] = normal
    moment_ref[RIGHT_AT:, :] = right

    if ends:
        moments = moment_ref[...]
        half = MOMENTS // 2
        packed = jnp.concatenate([moments[:half], moments[half:]], axis=1)
        for h in range(2):
            full[32 * h : 32 * h + 24, :] = packed[24 * h : 24 * h + 24]
            for r in range(4):
                at = 512 * h + 128 * r
                full[32 * h + 24 + r : 32 * h + 25 + r, :] = grad_ref[0:1, at : at + 128]
                full[32 * h + 28 + r : 32 * h + 29 + r, :] = grad_ref[1:2, at : at + 128]
        keep_ref[...] = full[pl.ds(pl.multiple_of(core[0] * 32, 32), 32), :]
        send_ref[...] = full[pl.ds(pl.multiple_of((1 - core[0]) * 32, 32), 32), :]


def chunk_terms(fill, start, count, first, marks, group_row, images, pieces, before=(), core=None):
    parts = marks.shape[0]
    begins = not before
    ends = core is not None
    operands = ([core] if ends else []) + [first, marks, group_row, *before, images, *pieces]
    large = 1 + len(pieces)
    specs = [SMEM if x.shape == (1,) else VMEM for x in operands[:-large]]
    specs += [pl.BlockSpec(memory_space=pl.ANY)] * large
    moments = jax.ShapeDtypeStruct((MOMENTS, GROUPS), F32)
    grads = jax.ShapeDtypeStruct((2, parts), F32)
    half = jax.ShapeDtypeStruct((32, 128), F32)
    work = [
        pltpu.VMEM((2048, 2 * count), BF16),
        pltpu.VMEM((parts, 2 * count), BF16),
        pltpu.VMEM((ROWS, 2048), BF16),
        pltpu.VMEM((GROUPS, 2 * count), F32),
        pltpu.VMEM((16, count), F32),
        pltpu.VMEM((RIGHT_AT, count), F32),
        pltpu.VMEM((ROWS, 2 * WIDE), F32),
        pltpu.VMEM((ROWS, 2 * WIDE), F32),
        pltpu.SemaphoreType.DMA((len(fill),)),
        pltpu.SemaphoreType.DMA((2,)),
    ]
    if ends:
        out_shape = [half, half]
        scratch = [pltpu.VMEM(moments.shape, F32), pltpu.VMEM(grads.shape, F32), pltpu.VMEM((64, 128), F32)] + work
    else:
        out_shape = [moments, grads]
        scratch = work
    spec = (fill, start, count, begins, ends)

    def body(*refs):
        chunk_kernel(spec, refs)

    return pl.pallas_call(
        body,
        in_specs=specs,
        out_specs=[VMEM, VMEM],
        out_shape=out_shape,
        scratch_shapes=scratch,
        compiler_params=params(),
        cost_estimate=pl.CostEstimate(
            flops=2 * parts * 2048 * 2 * count, bytes_accessed=4 * 1024 * 1024, transcendentals=0
        ),
        name="chunk_terms",
    )(*operands)


def whiten_kernel(core, own_ref, other_ref, white_ref, score_ref, both, rows):
    both[pl.ds(pl.multiple_of(core[0] * 32, 32), 32), :] = own_ref[...]
    both[pl.ds(pl.multiple_of((1 - core[0]) * 32, 32), 32), :] = other_ref[...]
    low = jnp.concatenate([both[0:24, :], both[32:56, :]], axis=0)
    moments = jnp.concatenate([low[:, :GROUPS], low[:, GROUPS:]], axis=0)
    at = 0
    rows[...] = jnp.zeros_like(rows)
    for j in range(ZERN):
        rows[j, j:ZERN, :] = moments[at : at + ZERN - j]
        at += ZERN - j
    right = moments[RIGHT_AT : RIGHT_AT + 16]
    line = [rows[j] for j in range(ZERN)]
    lane_row = lax.broadcasted_iota(jnp.int32, (16, GROUPS), 0)
    done = jnp.zeros((16, GROUPS), F32)
    for j in range(ZERN):
        inv = lax.rsqrt(line[j][j : j + 1] + RIDGE)
        col = line[j] * inv
        value = right[j : j + 1] * inv
        done = jnp.where(lane_row == j, value, done)
        right = right - col * value
        for i in range(j + 1, ZERN):
            line[i] = line[i] - col[i : i + 1] * col
    white_ref[...] = done[:ZERN]
    for h in range(2):
        grad = both[32 * h + 24 : 32 * h + 28, :]
        curv = both[32 * h + 28 : 32 * h + 32, :]
        score_ref[4 * h : 4 * h + 4, :] = -grad * lax.rsqrt(curv + 1e-06)


def spread(block, count):
    return jnp.broadcast_to(block[None], (count,) + block.shape)


def reduce_all(core, keep, send):
    mine = keep + lax.ppermute(send, "pix", CORE_SWAP)
    moments = jnp.sum(lax.all_to_all(spread(mine[:24], 8), "dom", 0, 0), axis=0)
    mine = jnp.concatenate([moments, mine[24:]], axis=0)
    mine = jnp.sum(lax.all_to_all(spread(mine, 16), "pix", 0, 0, axis_index_groups=CORE_GROUPS), axis=0)
    other = lax.ppermute(mine, "pix", CORE_SWAP)
    white, score = pl.pallas_call(
        whiten_kernel,
        in_specs=[SMEM, VMEM, VMEM],
        out_shape=[
            jax.ShapeDtypeStruct((ZERN, GROUPS), F32),
            jax.ShapeDtypeStruct((8, 128), F32),
        ],
        scratch_shapes=[pltpu.VMEM((64, 128), F32), pltpu.VMEM((ZERN, 16, GROUPS), F32)],
        name="whiten",
    )(core, mine, other)
    return white.T, score.reshape(-1)


def hop(block, perm):
    return lax.ppermute(block, "dom", perm)


def gate(*arrays):
    zero = jnp.zeros((), F32)
    for x in arrays:
        zero = zero + x[0, 0].astype(F32) * 0.0
    return zero.astype(BF16)


FILL_X_FIRST = [(0, 0, 0, 512), (1, 0, 1536, 512), (2, 0, 512, 512), (3, 0, 1024, 256), (4, 0, 1280, 256)]
FILL_Y_FIRST = [
    (0, 0, 0, 256),
    (0, 256, 1536, 256),
    (0, 512, 512, 256),
    (1, 0, 1024, 256),
    (2, 0, 256, 256),
    (2, 256, 1792, 256),
    (2, 512, 768, 256),
    (3, 0, 1280, 256),
]


def particle_marks(dom_at, class_of, pose_of, defocus, slot_class):
    slots = jnp.arange(8, dtype=jnp.int32)
    near = (((slots >> 1) - (dom_at >> 1)) & 3) * 2 + ((slots & 1) ^ (dom_at & 1))
    block = jnp.sum(jnp.where(slot_class[None, :] == class_of, near[None, :], 0), axis=1, dtype=jnp.int32)
    row = block * 256 + pose_of
    return jnp.stack([row.astype(F32), defocus.astype(F32)], axis=1)


def local(images, slices, class_of, pose_of, group_of, defocus, slot_class):
    parts, _, pix_count = images.shape
    poses = slices.shape[1]
    dom_at = lax.axis_index("dom").astype(jnp.int32)
    pix_at = lax.axis_index("pix").astype(jnp.int32)
    core = (pix_at & 1).reshape(1)
    first = (pix_at * pix_count).reshape(1)
    flat = slices.reshape(poses, 2 * pix_count)

    def own(start, count):
        return jnp.concatenate(
            [flat[:, start : start + count], flat[:, pix_count + start : pix_count + start + count]], axis=1
        )

    quarter = pix_count // 4
    at_b1, at_a1, at_b2, at_a2 = [quarter * i for i in range(4)]
    own_b1, own_a1, own_b2, own_a2 = [own(quarter * i, quarter) for i in range(4)]
    marks = particle_marks(dom_at, class_of, pose_of, defocus, slot_class)
    image_rows = images.reshape(parts, 2 * pix_count)
    shared = (first, marks, group_of[None, :], image_rows)

    b1_below = hop(own_b1, Y_UP)
    b1_above = hop(own_b1, Y_DOWN)
    a1_side = hop(own_a1, X_SWAP)
    a2_side = hop(own_a2, X_SWAP)
    start_2 = gate(b1_below, b1_above)
    b1_three = jnp.concatenate([own_b1, b1_below, b1_above], axis=0)
    b1_side_three = hop(b1_three, X_SWAP)
    b1_far_0 = hop(b1_below[:128] + gate(image_rows), Y_UP)
    b1_far_1 = hop(b1_above[128:] + gate(image_rows), Y_DOWN)
    own_b2 = own_b2 + start_2
    b2_below = hop(own_b2, Y_UP)
    b2_above = hop(own_b2, Y_DOWN)
    b1_far = jnp.concatenate([b1_far_0, b1_far_1], axis=0)
    b1_side_far = hop(b1_far, X_SWAP)
    a1_pair = jnp.concatenate([own_a1, a1_side], axis=0) + gate(a2_side, b1_far_0, b1_far_1)
    a1_below = hop(a1_pair, Y_UP)
    a1_above = hop(a1_pair, Y_DOWN)
    b2_three = jnp.concatenate([own_b2, b2_below, b2_above], axis=0)
    b2_side_three = hop(b2_three, X_SWAP)
    b2_far_0 = hop(b2_below[:128], Y_UP)
    b2_far_1 = hop(b2_above[128:], Y_DOWN)
    a1_far_0 = hop(a1_below[:256], Y_UP)
    a1_far_1 = hop(a1_above[256:], Y_DOWN)
    b2_far = jnp.concatenate([b2_far_0, b2_far_1], axis=0)
    b2_side_far = hop(b2_far, X_SWAP)
    a2_pair = jnp.concatenate([own_a2, a2_side], axis=0) + gate(a1_below, a1_above)
    a2_below = hop(a2_pair, Y_UP)
    a2_above = hop(a2_pair, Y_DOWN)

    sums = chunk_terms(FILL_Y_FIRST, at_b1, quarter, *shared, [b1_three, b1_far, b1_side_three, b1_side_far])
    sums = chunk_terms(
        FILL_X_FIRST, at_a1, quarter, *shared, [a1_pair, a1_below, a1_above, a1_far_0, a1_far_1], sums
    )
    late = gate(sums[0])
    a2_far_0 = hop(a2_below[:256] + late, Y_UP)
    a2_far_1 = hop(a2_above[256:] + late, Y_DOWN)
    sums = chunk_terms(
        FILL_Y_FIRST, at_b2, quarter, *shared, [b2_three, b2_far, b2_side_three, b2_side_far], sums
    )
    keep, send = chunk_terms(
        FILL_X_FIRST, at_a2, quarter, *shared, [a2_pair, a2_below, a2_above, a2_far_0, a2_far_1], sums, core
    )
    return reduce_all(core, keep, send)


def solution(mesh):
    return jax.shard_map(
        local,
        mesh=mesh,
        in_specs=(
            P("dom", None, "pix"),
            P("dom", None, None, "pix"),
            P("dom", None),
            P("dom"),
            P("dom"),
            P("dom"),
            P(),
        ),
        out_specs=(P(), P("dom")),
        check_vma=False,
    )
```

```python
import functools
import math

import jax
import jax.numpy as jnp
from jax import lax
from jax.experimental import pallas as pl
from jax.experimental.pallas import tpu as pltpu
from jax.sharding import PartitionSpec as P

BOX = 256
GROUPS = 64
ZERN = 12
PAIRS = ZERN * (ZERN + 1) // 2
PHASE_GAIN = 40.0
RIDGE = 1.0

WIDE = 256
MOMENTS = 96
RIGHT_AT = 80

SIN_POLY = (3.141592580044675, -5.167706878922935, 2.5500313772212047, -0.5980451737557255, 0.07722012821305138)
COS_POLY = (0.9999999534415752, -4.934792857330457, 4.058411894717311, -1.3318800570964462, 0.2196966127309024)

X_SWAP = [(d, d ^ 1) for d in range(8)]
Y_UP = [(d, (d + 2) % 8) for d in range(8)]
Y_DOWN = [(d, (d - 2) % 8) for d in range(8)]
CORE_SWAP = [(p, p ^ 1) for p in range(32)]
CORE_GROUPS = [[2 * m + c for m in range(16)] for c in range(2)]

F32 = jnp.float32
BF16 = jnp.bfloat16
SMEM = pl.BlockSpec(memory_space=pltpu.SMEM)
VMEM = pl.BlockSpec(memory_space=pltpu.VMEM)


def params():
    return pltpu.CompilerParams(vmem_limit_bytes=28 * 1024 * 1024)


def horner(coeffs, z):
    acc = jnp.full_like(z, coeffs[-1])
    for c in coeffs[-2::-1]:
        acc = acc * z + c
    return acc


STAGES = [(0, 4), (4, 7), (7, 8)]
NT = (((1,), (1,)), ((), ()))


def sort_kernel(place, slot_class, class_ref, pose_ref, group_ref, defocus_ref, image_ref, *refs):
    sorted_ref, perm_ref, col_ref, row_ref, count_ref, perm = refs
    parts = perm.shape[0]

    @pl.when(pl.program_id(0) == 0)
    def _():
        y0 = place[0] >> 1
        x0 = place[0] & 1
        cls = class_ref[...]
        block = jnp.zeros_like(cls)
        for slot in range(8):
            up = ((slot >> 1) - y0) & 3
            side = (slot & 1) ^ x0
            near = jnp.where(up == 3, 2, 3) + 2 * side
            at = jnp.where(up == 0, side, jnp.where(up == 2, 6 + side, near))
            block = jnp.where(cls == slot_class[slot], at, block)
        key = lax.broadcasted_iota(jnp.int32, (8, parts), 0)
        hot = jnp.where(key == block, 1.0, 0.0)
        sub = lax.broadcasted_iota(jnp.int32, (parts, parts), 0)
        lane = lax.broadcasted_iota(jnp.int32, (parts, parts), 1)
        perm[...] = jnp.where(sub < lane, 1.0, 0.0).astype(BF16)
        before = jnp.dot(hot.astype(BF16), perm[...], preferred_element_type=F32)
        total = jnp.sum(hot, axis=1, keepdims=True)
        rank = jnp.zeros((1, parts), F32)
        start = jnp.zeros((1, 1), F32)
        for k in range(8):
            rank = rank + hot[k : k + 1] * (before[k : k + 1] + start)
            start = start + total[k : k + 1]
        perm[...] = jnp.where(sub == rank.astype(jnp.int32), 1.0, 0.0).astype(BF16)
        perm_ref[...] = perm[...]
        mark = lax.broadcasted_iota(jnp.int32, (16, parts), 0)
        rows = jnp.where(mark == 0, block.astype(F32), 0.0)
        rows = jnp.where(mark == 1, pose_ref[...].astype(F32), rows)
        rows = jnp.where(mark == 2, defocus_ref[...], rows)
        rows = jnp.where(mark == 3, group_ref[...].astype(F32), rows).astype(BF16)
        col_ref[...] = lax.dot_general(perm[...], rows, NT, preferred_element_type=F32)
        row_ref[...] = lax.dot_general(rows, perm[...], NT, preferred_element_type=F32)
        for k in range(9):
            count_ref[k] = jnp.sum(jnp.where(block < k, 1.0, 0.0)).astype(jnp.int32)

    sorted_ref[...] = jnp.dot(perm[...], image_ref[...], preferred_element_type=F32).astype(BF16)


def sort_particles(place, slot_class, class_row, pose_row, group_row, defocus_row, images):
    parts, cols = images.shape
    row = pl.BlockSpec((1, parts), lambda i: (0, 0))
    return pl.pallas_call(
        sort_kernel,
        grid=(cols // 512,),
        in_specs=[SMEM, SMEM, row, row, row, row, pl.BlockSpec((parts, 512), lambda i: (0, i))],
        out_specs=[
            pl.BlockSpec((parts, 512), lambda i: (0, i)),
            pl.BlockSpec((parts, parts), lambda i: (0, 0)),
            pl.BlockSpec((parts, 16), lambda i: (0, 0)),
            pl.BlockSpec((16, parts), lambda i: (0, 0)),
            SMEM,
        ],
        out_shape=[
            jax.ShapeDtypeStruct((parts, cols), BF16),
            jax.ShapeDtypeStruct((parts, parts), BF16),
            jax.ShapeDtypeStruct((parts, 16), F32),
            jax.ShapeDtypeStruct((16, parts), F32),
            jax.ShapeDtypeStruct((9,), jnp.int32),
        ],
        scratch_shapes=[pltpu.VMEM((parts, parts), BF16)],
        compiler_params=params(),
        cost_estimate=pl.CostEstimate(
            flops=2 * parts * parts * cols, bytes_accessed=4 * parts * cols, transcendentals=0
        ),
        name="sort_particles",
    )(place, slot_class, class_row, pose_row, group_row, defocus_row, images)


def pixel_grid(first, count):
    index = first + lax.broadcasted_iota(jnp.int32, (1, count), 1)
    scale = math.sqrt(2.0) / BOX
    freq_x = (index & (BOX // 2 - 1)).astype(F32) * scale
    freq_y = ((index >> 7) - BOX // 2).astype(F32) * scale
    return freq_x, freq_y


def zernike_rows(freq_x, freq_y):
    q = freq_x * freq_x + freq_y * freq_y
    re1, im1 = freq_x, freq_y
    re2 = freq_x * freq_x - freq_y * freq_y
    im2 = 2.0 * freq_x * freq_y
    re3 = re2 * re1 - im2 * im1
    im3 = re2 * im1 + im2 * re1
    re5 = re3 * re2 - im3 * im2
    im5 = re3 * im2 + im3 * re2
    r3 = 3.0 * q - 2.0
    r5 = 10.0 * q * q - 12.0 * q + 3.0
    ro = 5.0 * q - 4.0
    return [re1, im1, r3 * re1, r3 * im1, r5 * re1, r5 * im1, re3, im3, ro * re3, ro * im3, re5, im5]


def row_range(stage, parts):
    return [(0, 768, 256), (256, parts, 256), (768, parts, 128)][stage]


def terms_kernel(stage, fill, refs):
    late = stage == 2
    refs = list(refs)
    core = refs.pop(0) if late else None
    first, counts, col_ref, row_ref = refs[:4]
    refs = refs[4:]
    if stage > 0:
        old_moments, old_grads = refs[:2]
        refs = refs[2:]
    image_ref = refs.pop(0)
    refs, work = refs[:-7], refs[-7:]
    table, image, sums, basis, pairs, table_sem, image_sem = work
    if late:
        keep_ref, send_ref, moment_ref, grad_ref, full = refs[-5:]
        pieces = refs[:-5]
    else:
        moment_ref, grad_ref, token_ref = refs[-3:]
        pieces = refs[:-3]
        token_ref[...] = jnp.zeros_like(token_ref)
    parts = col_ref.shape[0]
    pix_count = image_ref.shape[1] // 2
    kb_from, kb_to = STAGES[stage]
    row_from, row_to, tile = row_range(stage, parts)

    loads = []
    for i, (piece, src, src_col, dst, dst_col, rows, width) in enumerate(fill):
        loads.append(
            pltpu.make_async_copy(
                pieces[piece].at[pl.ds(src, rows), pl.ds(src_col, width)],
                table.at[pl.ds(dst, rows), pl.ds(dst_col, width)],
                table_sem.at[i],
            )
        )
    loads.append(
        pltpu.make_async_copy(image_ref.at[pl.ds(row_from, row_to - row_from), :], image, image_sem.at[0])
    )
    for copy in loads:
        copy.start()
    grad_ref[...] = old_grads[...] if stage > 0 else jnp.zeros_like(grad_ref)
    sums[...] = jnp.zeros_like(sums)
    freq_x, freq_y = pixel_grid(first[0], pix_count)
    q = freq_x * freq_x + freq_y * freq_y

    def lanes(v):
        return sum(v[:, 128 * i : 128 * i + 128] for i in range(v.shape[1] // 128))

    def work_on(at, rows):
        here = slice(at, at + rows)
        there = slice(at - row_from, at - row_from + rows)
        row = (col_ref[here, 0:1] * 256.0 + col_ref[here, 1:2]).astype(jnp.int32) - 256 * kb_from
        col = lax.broadcasted_iota(jnp.int32, (rows, 256 * (kb_to - kb_from)), 1)
        hot = jnp.where(col == row, 1.0, 0.0).astype(BF16)
        defocus = col_ref[here, 2:3] * (PHASE_GAIN / (2.0 * math.pi))
        group_hot = jnp.where(
            lax.broadcasted_iota(jnp.int32, (GROUPS, rows), 0) == row_ref[3:4, here].astype(jnp.int32), 1.0, 0.0
        ).astype(BF16)
        grad_sum = 0.0
        curv_sum = 0.0
        for pix in range(0, pix_count, WIDE):
            cols = slice(pix, pix + WIDE)
            other = slice(pix_count + pix, pix_count + pix + WIDE)
            proj_re = jnp.dot(hot, table[:, cols], preferred_element_type=F32)
            proj_im = jnp.dot(hot, table[:, other], preferred_element_type=F32)
            image_re = image[there, cols].astype(F32)
            image_im = image[there, other].astype(F32)
            q_sub = q[:, cols]

            turns = defocus * q_sub
            rest_turn = turns - jnp.floor(turns + 0.5)
            z = rest_turn * rest_turn
            s = rest_turn * horner(SIN_POLY, z)
            c = horner(COS_POLY, z)
            s2 = s + s
            sin_phi = s2 * c
            cos_phi = 1.0 - s2 * s

            power = proj_re * proj_re + proj_im * proj_im
            along = proj_re * image_re + proj_im * image_im
            across = proj_im * image_re - proj_re * image_im
            weight = (PHASE_GAIN * q_sub) * cos_phi
            sp = sin_phi * power
            grad_sum += lanes(weight * (sp + along))
            curv_sum += lanes(weight * weight * power)
            pred_power = sin_phi * sp
            cross = sin_phi * across

            cross_hi = cross.astype(BF16)
            cross_lo = (cross - cross_hi.astype(F32)).astype(BF16)
            sums[:, cols] += jnp.dot(group_hot, pred_power.astype(BF16), preferred_element_type=F32)
            sums[:, other] += jnp.dot(group_hot, cross_hi, preferred_element_type=F32) + jnp.dot(
                group_hot, cross_lo, preferred_element_type=F32
            )
        grad_ref[0:1, here] += jnp.sum(grad_sum.T, axis=0, keepdims=True)
        grad_ref[1:2, here] += jnp.sum(curv_sum.T, axis=0, keepdims=True)

    basis[...] = jnp.zeros_like(basis)
    for j, row in enumerate(zernike_rows(freq_x, freq_y)):
        basis[j : j + 1, :] = row
    pairs[72:80, :] = jnp.zeros((8, pix_count), F32)
    at = 0
    for j in range(ZERN):
        pairs[at : at + ZERN - j, :] = basis[j : j + 1, :] * basis[j:ZERN, :]
        at += ZERN - j

    for copy in loads:
        copy.wait()
    for at in range(row_from, row_to, tile):
        some = (counts[kb_from] < at + tile) & (counts[kb_to] > at)
        pl.when(some)(functools.partial(work_on, at, tile))

    normal = lax.dot_general(
        pairs[...], sums[:, :pix_count], NT, precision=lax.Precision.HIGHEST, preferred_element_type=F32
    )
    right = lax.dot_general(
        basis[...], sums[:, pix_count:], NT, precision=lax.Precision.HIGHEST, preferred_element_type=F32
    )
    if stage > 0:
        normal = normal + old_moments[0:RIGHT_AT, :]
        right = right + old_moments[RIGHT_AT:, :]
    moment_ref[0:RIGHT_AT, :] = normal
    moment_ref[RIGHT_AT:, :] = right

    if late:
        grads = grad_ref[...]
        moments = moment_ref[...]
        packed = jnp.concatenate([moments[: MOMENTS // 2], moments[MOMENTS // 2 :]], axis=1)
        for h in range(2):
            full[32 * h : 32 * h + 24, :] = packed[24 * h : 24 * h + 24]
            for r in range(4):
                at = 512 * h + 128 * r
                full[32 * h + 24 + r : 32 * h + 25 + r, :] = grads[0:1, at : at + 128]
                full[32 * h + 28 + r : 32 * h + 29 + r, :] = grads[1:2, at : at + 128]
        keep_ref[...] = full[pl.ds(pl.multiple_of(core[0] * 32, 32), 32), :]
        send_ref[...] = full[pl.ds(pl.multiple_of((1 - core[0]) * 32, 32), 32), :]


def particle_terms(stage, fill, first, counts, mark_cols, mark_rows, images, pieces, before=(), core=None):
    parts = mark_cols.shape[0]
    pix_count = images.shape[1] // 2
    late = stage == 2
    operands = [first, counts, mark_cols, mark_rows, *before]
    specs = [SMEM, SMEM] + [VMEM] * (2 + len(before))
    if late:
        operands = [core] + operands
        specs = [SMEM] + specs
    operands += [images, *pieces]
    specs += [pl.BlockSpec(memory_space=pltpu.HBM)] + [pl.BlockSpec(memory_space=pl.ANY)] * len(pieces)
    moments = jax.ShapeDtypeStruct((MOMENTS, GROUPS), F32)
    grads = jax.ShapeDtypeStruct((2, parts), F32)
    half = jax.ShapeDtypeStruct((32, 128), F32)
    kb_from, kb_to = STAGES[stage]
    row_from, row_to, _ = row_range(stage, parts)
    work = [
        pltpu.VMEM((256 * (kb_to - kb_from), 2 * pix_count), BF16),
        pltpu.VMEM((row_to - row_from, 2 * pix_count), BF16),
        pltpu.VMEM((GROUPS, 2 * pix_count), F32),
        pltpu.VMEM((16, pix_count), F32),
        pltpu.VMEM((RIGHT_AT, pix_count), F32),
        pltpu.SemaphoreType.DMA((len(fill),)),
        pltpu.SemaphoreType.DMA((1,)),
    ]
    if late:
        out_shape = [half, half]
        scratch = [
            pltpu.VMEM(moments.shape, F32),
            pltpu.VMEM(grads.shape, F32),
            pltpu.VMEM((64, 128), F32),
        ] + work
    else:
        out_shape = [moments, grads, jax.ShapeDtypeStruct((16, pix_count), BF16)]
        scratch = work

    def body(*refs):
        terms_kernel(stage, fill, refs)

    return pl.pallas_call(
        body,
        in_specs=specs,
        out_specs=[VMEM] * len(out_shape),
        out_shape=out_shape,
        scratch_shapes=scratch,
        compiler_params=params(),
        cost_estimate=pl.CostEstimate(
            flops=[4, 3, 1][stage] * 2 * parts * 2048 * pix_count,
            bytes_accessed=8 * 1024 * 1024,
            transcendentals=0,
        ),
        name="terms_%d" % stage,
    )(*operands)


def whiten_kernel(core, own_ref, other_ref, perm_ref, white_ref, score_ref, both, rows, perm, perm_sem, split):
    perm_load = pltpu.make_async_copy(perm_ref, perm, perm_sem.at[0])
    perm_load.start()
    both[pl.ds(pl.multiple_of(core[0] * 32, 32), 32), :] = own_ref[...]
    both[pl.ds(pl.multiple_of((1 - core[0]) * 32, 32), 32), :] = other_ref[...]
    low = jnp.concatenate([both[0:24, :], both[32:56, :]], axis=0)
    moments = jnp.concatenate([low[:, :GROUPS], low[:, GROUPS:]], axis=0)
    at = 0
    rows[...] = jnp.zeros_like(rows)
    for j in range(ZERN):
        rows[j, j:ZERN, :] = moments[at : at + ZERN - j]
        at += ZERN - j
    right = moments[RIGHT_AT : RIGHT_AT + 16]
    line = [rows[j] for j in range(ZERN)]
    lane_row = lax.broadcasted_iota(jnp.int32, (16, GROUPS), 0)
    done = jnp.zeros((16, GROUPS), F32)
    for j in range(ZERN):
        inv = lax.rsqrt(line[j][j : j + 1] + RIDGE)
        col = line[j] * inv
        value = right[j : j + 1] * inv
        done = jnp.where(lane_row == j, value, done)
        right = right - col * value
        for i in range(j + 1, ZERN):
            line[i] = line[i] - col[i : i + 1] * col
    white_ref[...] = done[:ZERN]
    split[...] = jnp.zeros_like(split)
    for h in range(2):
        grad = both[32 * h + 24 : 32 * h + 28, :]
        curv = both[32 * h + 28 : 32 * h + 32, :]
        score = -grad * lax.rsqrt(curv + 1e-06)
        for r in range(4):
            at = 512 * h + 128 * r
            rest = score[r : r + 1]
            for k in range(3):
                term = rest.astype(BF16).astype(F32)
                split[k : k + 1, at : at + 128] = term
                rest = rest - term
    perm_load.wait()
    back = jnp.dot(split[...].astype(BF16), perm[...], preferred_element_type=F32)
    score_ref[...] = back[0:1] + back[1:2] + back[2:3]


def spread(block, count):
    return jnp.broadcast_to(block[None], (count,) + block.shape)


def reduce_all(core, keep, send, perm):
    mine = keep + lax.ppermute(send, "pix", CORE_SWAP)
    moments = jnp.sum(lax.all_to_all(spread(mine[:24], 8), "dom", 0, 0), axis=0)
    mine = jnp.concatenate([moments, mine[24:]], axis=0)
    mine = jnp.sum(lax.all_to_all(spread(mine, 16), "pix", 0, 0, axis_index_groups=CORE_GROUPS), axis=0)
    other = lax.ppermute(mine, "pix", CORE_SWAP)
    white, score = pl.pallas_call(
        whiten_kernel,
        in_specs=[SMEM, VMEM, VMEM, pl.BlockSpec(memory_space=pltpu.HBM)],
        out_shape=[
            jax.ShapeDtypeStruct((ZERN, GROUPS), F32),
            jax.ShapeDtypeStruct((1, perm.shape[0]), F32),
        ],
        scratch_shapes=[
            pltpu.VMEM((64, 128), F32),
            pltpu.VMEM((ZERN, 16, GROUPS), F32),
            pltpu.VMEM(perm.shape, BF16),
            pltpu.SemaphoreType.DMA((1,)),
            pltpu.VMEM((16, perm.shape[0]), F32),
        ],
        name="whiten",
    )(core, mine, other, perm)
    return white.T, score.reshape(-1)


def hop(block, perm):
    return lax.ppermute(block, "dom", perm)


def fills(pix_count):
    half = pix_count // 2

    def parted(piece, src, dst, rows, at):
        return [(piece, src, part * half, dst, part * pix_count + at, rows, half) for part in range(2)]

    own = [(piece, 0, 0, 256 * piece, 0, 256, 2 * pix_count) for piece in range(4)]
    next_a = parted(0, 0, 0, 256, 0) + parted(1, 0, 256, 256, 0)
    next_b = parted(2, 0, 0, 512, half)
    far = parted(0, 256, 512, 128, 0) + parted(1, 256, 640, 128, 0)
    far += parted(0, 384, 512, 128, half) + parted(1, 384, 640, 128, half)
    last = parted(0, 0, 0, 128, 0) + parted(1, 0, 128, 128, 0) + parted(2, 0, 0, 256, half)
    return [own, next_a + next_b + far, last]


def local(images, slices, class_of, pose_of, group_of, defocus, slot_class):
    parts, _, pix_count = images.shape
    poses = slices.shape[1]
    dom_at = lax.axis_index("dom").astype(jnp.int32).reshape(1)
    pix_at = lax.axis_index("pix").astype(jnp.int32)
    core = (pix_at & 1).reshape(1)
    first = (pix_at * pix_count).reshape(1)
    half = pix_count // 2
    flat = slices.reshape(poses, 2 * pix_count)

    def rows(*blocks):
        return jnp.concatenate(blocks, axis=0)

    def cols(*blocks):
        return jnp.concatenate(blocks, axis=1)

    def part_a(block):
        return cols(block[:, :half], block[:, pix_count : pix_count + half])

    def part_b(block):
        return cols(block[:, half:pix_count], block[:, pix_count + half :])

    side = hop(flat, X_SWAP)
    below = hop(flat, Y_UP)
    above = hop(flat, Y_DOWN)
    image_rows, perm, mark_cols, mark_rows, counts = sort_particles(
        dom_at,
        slot_class,
        class_of.reshape(1, parts),
        pose_of[None, :],
        group_of[None, :],
        defocus.astype(F32)[None, :],
        images.reshape(parts, 2 * pix_count),
    )

    up = hop(rows(part_a(side), part_a(below[:128]), part_b(below[:128])), Y_UP)
    down = hop(rows(part_a(side), part_a(above[128:]), part_b(above[128:]), image_rows[:16, :pix_count]), Y_DOWN)
    b_side = hop(rows(part_b(below), part_b(above)), X_SWAP)
    fill = fills(pix_count)
    shared = (first, counts, mark_cols, mark_rows, image_rows)
    *sums, token = particle_terms(0, fill[0], *shared, [flat, side, below, above])

    far_a_0 = hop(up[:128], Y_UP)
    far_a_1 = hop(down[128:256], Y_DOWN)
    far_b = hop(rows(up[384:512], down[384:512], token), X_SWAP)
    *sums, _ = particle_terms(1, fill[1], *shared, [up, down, b_side], sums)
    keep, send = particle_terms(2, fill[2], *shared, [far_a_0, far_a_1, far_b], sums, core)
    return reduce_all(core, keep, send, perm)


def solution(mesh):
    return jax.shard_map(
        local,
        mesh=mesh,
        in_specs=(
            P("dom", None, "pix"),
            P("dom", None, None, "pix"),
            P("dom", None),
            P("dom"),
            P("dom"),
            P("dom"),
            P(),
        ),
        out_specs=(P(), P("dom")),
        check_vma=False,
    )
```

```python
import functools
import math

import jax
import jax.numpy as jnp
from jax import lax
from jax.experimental import pallas as pl
from jax.experimental.pallas import tpu as pltpu
from jax.sharding import PartitionSpec as P

BOX = 256
GROUPS = 64
ZERN = 12
PAIRS = ZERN * (ZERN + 1) // 2
PHASE_GAIN = 40.0
RIDGE = 1.0

WIDE = 256
MOMENTS = 96
RIGHT_AT = 80

SIN_POLY = (3.141592580044675, -5.167706878922935, 2.5500313772212047, -0.5980451737557255, 0.07722012821305138)
COS_POLY = (0.9999999534415752, -4.934792857330457, 4.058411894717311, -1.3318800570964462, 0.2196966127309024)

X_SWAP = [(d, d ^ 1) for d in range(8)]
Y_UP = [(d, (d + 2) % 8) for d in range(8)]
Y_DOWN = [(d, (d - 2) % 8) for d in range(8)]
CORE_SWAP = [(p, p ^ 1) for p in range(32)]
CORE_GROUPS = [[2 * m + c for m in range(16)] for c in range(2)]

F32 = jnp.float32
BF16 = jnp.bfloat16
SMEM = pl.BlockSpec(memory_space=pltpu.SMEM)
VMEM = pl.BlockSpec(memory_space=pltpu.VMEM)


def params():
    return pltpu.CompilerParams(vmem_limit_bytes=16 * 1024 * 1024)


def horner(coeffs, z):
    acc = jnp.full_like(z, coeffs[-1])
    for c in coeffs[-2::-1]:
        acc = acc * z + c
    return acc


STAGES = [(0, 4), (4, 7), (7, 8)]
NT = (((1,), (1,)), ((), ()))


def sort_kernel(place, slot_class, class_ref, pose_ref, group_ref, defocus_ref, image_ref, *refs):
    sorted_ref, perm_ref, col_ref, row_ref, count_ref, perm = refs
    parts = perm.shape[0]

    @pl.when(pl.program_id(0) == 0)
    def _():
        y0 = place[0] >> 1
        x0 = place[0] & 1
        cls = class_ref[...]
        block = jnp.zeros_like(cls)
        for slot in range(8):
            up = ((slot >> 1) - y0) & 3
            side = (slot & 1) ^ x0
            near = jnp.where(up == 3, 2, 3) + 2 * side
            at = jnp.where(up == 0, side, jnp.where(up == 2, 6 + side, near))
            block = jnp.where(cls == slot_class[slot], at, block)
        key = lax.broadcasted_iota(jnp.int32, (8, parts), 0)
        hot = jnp.where(key == block, 1.0, 0.0)
        sub = lax.broadcasted_iota(jnp.int32, (parts, parts), 0)
        lane = lax.broadcasted_iota(jnp.int32, (parts, parts), 1)
        perm[...] = jnp.where(sub < lane, 1.0, 0.0).astype(BF16)
        before = jnp.dot(hot.astype(BF16), perm[...], preferred_element_type=F32)
        total = jnp.sum(hot, axis=1, keepdims=True)
        rank = jnp.zeros((1, parts), F32)
        start = jnp.zeros((1, 1), F32)
        for k in range(8):
            rank = rank + hot[k : k + 1] * (before[k : k + 1] + start)
            start = start + total[k : k + 1]
        perm[...] = jnp.where(sub == rank.astype(jnp.int32), 1.0, 0.0).astype(BF16)
        perm_ref[...] = perm[...]
        mark = lax.broadcasted_iota(jnp.int32, (16, parts), 0)
        rows = jnp.where(mark == 0, block.astype(F32), 0.0)
        rows = jnp.where(mark == 1, pose_ref[...].astype(F32), rows)
        rows = jnp.where(mark == 2, defocus_ref[...], rows)
        rows = jnp.where(mark == 3, group_ref[...].astype(F32), rows).astype(BF16)
        col_ref[...] = lax.dot_general(perm[...], rows, NT, preferred_element_type=F32)
        row_ref[...] = lax.dot_general(rows, perm[...], NT, preferred_element_type=F32)
        for k in range(9):
            count_ref[k] = jnp.sum(jnp.where(block < k, 1.0, 0.0)).astype(jnp.int32)

    sorted_ref[...] = jnp.dot(perm[...], image_ref[...], preferred_element_type=F32).astype(BF16)


def sort_particles(place, slot_class, class_row, pose_row, group_row, defocus_row, images):
    parts, cols = images.shape
    row = pl.BlockSpec((1, parts), lambda i: (0, 0))
    return pl.pallas_call(
        sort_kernel,
        grid=(cols // 512,),
        in_specs=[SMEM, SMEM, row, row, row, row, pl.BlockSpec((parts, 512), lambda i: (0, i))],
        out_specs=[
            pl.BlockSpec((parts, 512), lambda i: (0, i)),
            pl.BlockSpec((parts, parts), lambda i: (0, 0)),
            pl.BlockSpec((parts, 16), lambda i: (0, 0)),
            pl.BlockSpec((16, parts), lambda i: (0, 0)),
            SMEM,
        ],
        out_shape=[
            pltpu.HBM((parts, cols), BF16),
            pltpu.HBM((parts, parts), BF16),
            jax.ShapeDtypeStruct((parts, 16), F32),
            jax.ShapeDtypeStruct((16, parts), F32),
            jax.ShapeDtypeStruct((9,), jnp.int32),
        ],
        scratch_shapes=[pltpu.VMEM((parts, parts), BF16)],
        compiler_params=params(),
        cost_estimate=pl.CostEstimate(
            flops=2 * parts * parts * cols, bytes_accessed=4 * parts * cols, transcendentals=0
        ),
        name="sort_particles",
    )(place, slot_class, class_row, pose_row, group_row, defocus_row, images)


def pixel_grid(first, count):
    index = first + lax.broadcasted_iota(jnp.int32, (1, count), 1)
    scale = math.sqrt(2.0) / BOX
    freq_x = (index & (BOX // 2 - 1)).astype(F32) * scale
    freq_y = ((index >> 7) - BOX // 2).astype(F32) * scale
    return freq_x, freq_y


def zernike_rows(freq_x, freq_y):
    q = freq_x * freq_x + freq_y * freq_y
    re1, im1 = freq_x, freq_y
    re2 = freq_x * freq_x - freq_y * freq_y
    im2 = 2.0 * freq_x * freq_y
    re3 = re2 * re1 - im2 * im1
    im3 = re2 * im1 + im2 * re1
    re5 = re3 * re2 - im3 * im2
    im5 = re3 * im2 + im3 * re2
    r3 = 3.0 * q - 2.0
    r5 = 10.0 * q * q - 12.0 * q + 3.0
    ro = 5.0 * q - 4.0
    return [re1, im1, r3 * re1, r3 * im1, r5 * re1, r5 * im1, re3, im3, ro * re3, ro * im3, re5, im5]


def row_range(stage, parts):
    return [(0, 768, 256), (256, parts, 256), (832, parts, 192)][stage]


def terms_kernel(stage, fill, refs):
    late = stage == 2
    refs = list(refs)
    core = refs.pop(0) if late else None
    first, counts, col_ref, row_ref = refs[:4]
    refs = refs[4:]
    if stage > 0:
        old_moments, old_grads = refs[:2]
        refs = refs[2:]
    image_ref = refs.pop(0)
    refs, work = refs[:-7], refs[-7:]
    table, image, sums, basis, pairs, table_sem, image_sem = work
    if late:
        keep_ref, send_ref, grad_ref, moment_ref, full = refs[-5:]
        pieces = refs[:-5]
    else:
        moment_ref, grad_ref, token_ref = refs[-3:]
        pieces = refs[:-3]
        token_ref[...] = jnp.zeros_like(token_ref)
    parts = col_ref.shape[0]
    pix_count = image_ref.shape[1] // 2
    kb_from, kb_to = STAGES[stage]
    row_from, row_to, tile = row_range(stage, parts)

    loads = []
    for i, (piece, src, src_col, dst, dst_col, rows, width) in enumerate(fill):
        loads.append(
            pltpu.make_async_copy(
                pieces[piece].at[pl.ds(src, rows), pl.ds(src_col, width)],
                table.at[pl.ds(dst, rows), pl.ds(dst_col, width)],
                table_sem.at[i],
            )
        )
    loads.append(
        pltpu.make_async_copy(image_ref.at[pl.ds(row_from, row_to - row_from), :], image, image_sem.at[0])
    )
    for copy in loads:
        copy.start()
    grad_ref[...] = old_grads[...] if stage > 0 else jnp.zeros_like(grad_ref)
    sums[...] = jnp.zeros_like(sums)
    freq_x, freq_y = pixel_grid(first[0], pix_count)
    q = freq_x * freq_x + freq_y * freq_y

    def lanes(v):
        return sum(v[:, 128 * i : 128 * i + 128] for i in range(v.shape[1] // 128))

    def work_on(at, rows):
        here = slice(at, at + rows)
        there = slice(at - row_from, at - row_from + rows)
        row = (col_ref[here, 0:1] * 256.0 + col_ref[here, 1:2]).astype(jnp.int32) - 256 * kb_from
        col = lax.broadcasted_iota(jnp.int32, (rows, 256 * (kb_to - kb_from)), 1)
        hot = jnp.where(col == row, 1.0, 0.0).astype(BF16)
        defocus = col_ref[here, 2:3] * (PHASE_GAIN / (2.0 * math.pi))
        group_hot = jnp.where(
            lax.broadcasted_iota(jnp.int32, (GROUPS, rows), 0) == row_ref[3:4, here].astype(jnp.int32), 1.0, 0.0
        ).astype(BF16)
        grad_sum = 0.0
        curv_sum = 0.0
        for pix in range(0, pix_count, WIDE):
            cols = slice(pix, pix + WIDE)
            other = slice(pix_count + pix, pix_count + pix + WIDE)
            proj_re = jnp.dot(hot, table[:, cols], preferred_element_type=F32)
            proj_im = jnp.dot(hot, table[:, other], preferred_element_type=F32)
            image_re = image[there, cols].astype(F32)
            image_im = image[there, other].astype(F32)
            q_sub = q[:, cols]

            turns = defocus * q_sub
            rest_turn = turns - jnp.floor(turns + 0.5)
            z = rest_turn * rest_turn
            s = rest_turn * horner(SIN_POLY, z)
            c = horner(COS_POLY, z)
            s2 = s + s
            sin_phi = s2 * c
            cos_phi = 1.0 - s2 * s

            power = proj_re * proj_re + proj_im * proj_im
            along = proj_re * image_re + proj_im * image_im
            across = proj_im * image_re - proj_re * image_im
            weight = (PHASE_GAIN * q_sub) * cos_phi
            sp = sin_phi * power
            grad_sum += lanes(weight * (sp + along))
            curv_sum += lanes(weight * weight * power)
            pred_power = sin_phi * sp
            cross = sin_phi * across

            cross_hi = cross.astype(BF16)
            cross_lo = (cross - cross_hi.astype(F32)).astype(BF16)
            sums[:, cols] += jnp.dot(group_hot, pred_power.astype(BF16), preferred_element_type=F32)
            sums[:, other] += jnp.dot(group_hot, cross_hi, preferred_element_type=F32) + jnp.dot(
                group_hot, cross_lo, preferred_element_type=F32
            )
        grad_ref[0:1, here] += jnp.sum(grad_sum.T, axis=0, keepdims=True)
        grad_ref[1:2, here] += jnp.sum(curv_sum.T, axis=0, keepdims=True)

    basis[...] = jnp.zeros_like(basis)
    for j, row in enumerate(zernike_rows(freq_x, freq_y)):
        basis[j : j + 1, :] = row
    pairs[72:80, :] = jnp.zeros((8, pix_count), F32)
    at = 0
    for j in range(ZERN):
        pairs[at : at + ZERN - j, :] = basis[j : j + 1, :] * basis[j:ZERN, :]
        at += ZERN - j

    for copy in loads:
        copy.wait()
    for at in range(row_from, row_to, tile):
        some = (counts[kb_from] < at + tile) & (counts[kb_to] > at)
        pl.when(some)(functools.partial(work_on, at, tile))

    normal = lax.dot_general(
        pairs[...], sums[:, :pix_count], NT, precision=lax.Precision.HIGHEST, preferred_element_type=F32
    )
    right = lax.dot_general(
        basis[...], sums[:, pix_count:], NT, precision=lax.Precision.HIGHEST, preferred_element_type=F32
    )
    if stage > 0:
        normal = normal + old_moments[0:RIGHT_AT, :]
        right = right + old_moments[RIGHT_AT:, :]
    moment_ref[0:RIGHT_AT, :] = normal
    moment_ref[RIGHT_AT:, :] = right

    if late:
        moments = moment_ref[...]
        full[...] = jnp.concatenate([moments[: MOMENTS // 2], moments[MOMENTS // 2 :]], axis=1)
        keep_ref[...] = full[pl.ds(pl.multiple_of(core[0] * 24, 8), 24), :]
        send_ref[...] = full[pl.ds(pl.multiple_of((1 - core[0]) * 24, 8), 24), :]


def particle_terms(stage, fill, first, counts, mark_cols, mark_rows, images, pieces, before=(), core=None):
    parts = mark_cols.shape[0]
    pix_count = images.shape[1] // 2
    late = stage == 2
    operands = [first, counts, mark_cols, mark_rows, *before]
    specs = [SMEM, SMEM] + [VMEM] * (2 + len(before))
    if late:
        operands = [core] + operands
        specs = [SMEM] + specs
    operands += [images, *pieces]
    specs += [pl.BlockSpec(memory_space=pltpu.HBM)] + [pl.BlockSpec(memory_space=pl.ANY)] * len(pieces)
    moments = jax.ShapeDtypeStruct((MOMENTS, GROUPS), F32)
    grads = jax.ShapeDtypeStruct((2, parts), F32)
    half = jax.ShapeDtypeStruct((24, 128), F32)
    kb_from, kb_to = STAGES[stage]
    row_from, row_to, _ = row_range(stage, parts)
    work = [
        pltpu.VMEM((256 * (kb_to - kb_from), 2 * pix_count), BF16),
        pltpu.VMEM((row_to - row_from, 2 * pix_count), BF16),
        pltpu.VMEM((GROUPS, 2 * pix_count), F32),
        pltpu.VMEM((16, pix_count), F32),
        pltpu.VMEM((RIGHT_AT, pix_count), F32),
        pltpu.SemaphoreType.DMA((len(fill),)),
        pltpu.SemaphoreType.DMA((1,)),
    ]
    if late:
        out_shape = [half, half, grads]
        scratch = [pltpu.VMEM(moments.shape, F32), pltpu.VMEM((48, 128), F32)] + work
    else:
        out_shape = [moments, grads, jax.ShapeDtypeStruct((16, pix_count), BF16)]
        scratch = work

    def body(*refs):
        terms_kernel(stage, fill, refs)

    return pl.pallas_call(
        body,
        in_specs=specs,
        out_specs=[VMEM] * len(out_shape),
        out_shape=out_shape,
        scratch_shapes=scratch,
        compiler_params=params(),
        cost_estimate=pl.CostEstimate(
            flops=[4, 3, 1][stage] * 2 * parts * 2048 * pix_count,
            bytes_accessed=8 * 1024 * 1024,
            transcendentals=0,
        ),
        name="terms_%d" % stage,
    )(*operands)


def unsort_kernel(core, grad_ref, perm_ref, keep_ref, send_ref, split, full, perm, perm_sem):
    perm_load = pltpu.make_async_copy(perm_ref, perm, perm_sem.at[0])
    perm_load.start()
    rest = grad_ref[...]
    split[...] = jnp.zeros_like(split)
    for k in range(3):
        term = rest.astype(BF16).astype(F32)
        split[2 * k : 2 * k + 2, :] = term
        rest = rest - term
    perm_load.wait()
    back = jnp.dot(split[...].astype(BF16), perm[...], preferred_element_type=F32)
    grads = back[0:2] + back[2:4] + back[4:6]
    for h in range(2):
        for r in range(4):
            at = 512 * h + 128 * r
            full[8 * h + r : 8 * h + r + 1, :] = grads[0:1, at : at + 128]
            full[8 * h + 4 + r : 8 * h + 5 + r, :] = grads[1:2, at : at + 128]
    keep_ref[...] = full[pl.ds(pl.multiple_of(core[0] * 8, 8), 8), :]
    send_ref[...] = full[pl.ds(pl.multiple_of((1 - core[0]) * 8, 8), 8), :]


def unsort(core, grads, perm):
    half = jax.ShapeDtypeStruct((8, 128), F32)
    return pl.pallas_call(
        unsort_kernel,
        in_specs=[SMEM, VMEM, pl.BlockSpec(memory_space=pltpu.HBM)],
        out_shape=[half, half],
        scratch_shapes=[
            pltpu.VMEM((16, perm.shape[0]), F32),
            pltpu.VMEM((16, 128), F32),
            pltpu.VMEM(perm.shape, BF16),
            pltpu.SemaphoreType.DMA((1,)),
        ],
        compiler_params=params(),
        name="unsort",
    )(core, grads, perm)


def whiten_kernel(core, own_ref, other_ref, white_ref, score_ref, both, rows, sem):
    loads = [
        pltpu.make_async_copy(ref, both.at[pl.ds(pl.multiple_of(at * 32, 32), 32), :], sem.at[i])
        for i, (ref, at) in enumerate([(own_ref, core[0]), (other_ref, 1 - core[0])])
    ]
    for copy in loads:
        copy.start()
    for copy in loads:
        copy.wait()
    low = jnp.concatenate([both[0:24, :], both[32:56, :]], axis=0)
    moments = jnp.concatenate([low[:, :GROUPS], low[:, GROUPS:]], axis=0)
    at = 0
    rows[...] = jnp.zeros_like(rows)
    for j in range(ZERN):
        rows[j, j:ZERN, :] = moments[at : at + ZERN - j]
        at += ZERN - j
    right = moments[RIGHT_AT : RIGHT_AT + 16]
    line = [rows[j] for j in range(ZERN)]
    lane_row = lax.broadcasted_iota(jnp.int32, (16, GROUPS), 0)
    done = jnp.zeros((16, GROUPS), F32)
    for j in range(ZERN):
        inv = lax.rsqrt(line[j][j : j + 1] + RIDGE)
        col = line[j] * inv
        value = right[j : j + 1] * inv
        done = jnp.where(lane_row == j, value, done)
        right = right - col * value
        for i in range(j + 1, ZERN):
            line[i] = line[i] - col[i : i + 1] * col
    white_ref[...] = done[:ZERN]
    for h in range(2):
        grad = both[32 * h + 24 : 32 * h + 28, :]
        curv = both[32 * h + 28 : 32 * h + 32, :]
        score_ref[4 * h : 4 * h + 4, :] = -grad * lax.rsqrt(curv + 1e-06)


def spread(block, count):
    return jnp.broadcast_to(block[None], (count,) + block.shape)


def reduce_all(core, keep, send, grads, perm):
    mine = keep + lax.ppermute(send, "pix", CORE_SWAP)
    moments = jnp.sum(lax.all_to_all(spread(mine, 8), "dom", 0, 0), axis=0)
    keep, send = unsort(core, grads, perm)
    grads = keep + lax.ppermute(send, "pix", CORE_SWAP)
    mine = jnp.concatenate([moments, grads], axis=0)
    mine = jnp.sum(lax.all_to_all(spread(mine, 16), "pix", 0, 0, axis_index_groups=CORE_GROUPS), axis=0)
    other = lax.ppermute(mine, "pix", CORE_SWAP)
    white, score = pl.pallas_call(
        whiten_kernel,
        in_specs=[SMEM] + [pl.BlockSpec(memory_space=pl.ANY)] * 2,
        out_shape=[
            jax.ShapeDtypeStruct((ZERN, GROUPS), F32),
            jax.ShapeDtypeStruct((8, 128), F32),
        ],
        scratch_shapes=[
            pltpu.VMEM((64, 128), F32),
            pltpu.VMEM((ZERN, 16, GROUPS), F32),
            pltpu.SemaphoreType.DMA((2,)),
        ],
        compiler_params=params(),
        name="whiten",
    )(core, mine, other)
    return white.T, score.reshape(-1)


def hop(block, perm):
    return lax.ppermute(block, "dom", perm)


def fills(pix_count):
    half = pix_count // 2

    def parted(piece, src, dst, rows, at):
        return [(piece, src, part * half, dst, part * pix_count + at, rows, half) for part in range(2)]

    own = [(piece, 0, 0, 256 * piece, 0, 256, 2 * pix_count) for piece in range(4)]
    next_a = parted(0, 0, 0, 256, 0) + parted(1, 0, 256, 256, 0)
    next_b = parted(2, 0, 0, 512, half)
    far = parted(0, 256, 512, 128, 0) + parted(1, 256, 640, 128, 0)
    far += parted(0, 384, 512, 128, half) + parted(1, 384, 640, 128, half)
    last = parted(0, 0, 0, 256, half) + parted(1, 0, 0, 128, 0) + parted(2, 0, 128, 128, 0)
    return [own, next_a + next_b + far, last]


def local(images, slices, class_of, pose_of, group_of, defocus, slot_class):
    parts, _, pix_count = images.shape
    poses = slices.shape[1]
    dom_at = lax.axis_index("dom").astype(jnp.int32).reshape(1)
    pix_at = lax.axis_index("pix").astype(jnp.int32)
    core = (pix_at & 1).reshape(1)
    first = (pix_at * pix_count).reshape(1)
    half = pix_count // 2
    flat = slices.reshape(poses, 2 * pix_count)

    def rows(*blocks):
        return jnp.concatenate(blocks, axis=0)

    def cols(*blocks):
        return jnp.concatenate(blocks, axis=1)

    def part_a(block):
        return cols(block[:, :half], block[:, pix_count : pix_count + half])

    def part_b(block):
        return cols(block[:, half:pix_count], block[:, pix_count + half :])

    side = hop(flat, X_SWAP)
    below = hop(flat, Y_UP)
    above = hop(flat, Y_DOWN)
    image_rows, perm, mark_cols, mark_rows, counts = sort_particles(
        dom_at,
        slot_class,
        class_of.reshape(1, parts),
        pose_of[None, :],
        group_of[None, :],
        defocus.astype(F32)[None, :],
        images.reshape(parts, 2 * pix_count),
    )

    up = hop(rows(part_a(side), part_a(below[:128]), part_b(below[:128])), Y_UP)
    down = hop(rows(part_a(side), part_a(above[128:]), part_b(above[128:]), image_rows[:16, :pix_count]), Y_DOWN)
    b_side = hop(rows(part_b(below), part_b(above)), X_SWAP)
    fill = fills(pix_count)
    shared = (first, counts, mark_cols, mark_rows, image_rows)
    *sums, token = particle_terms(0, fill[0], *shared, [flat, side, below, above])

    far_a_0 = hop(up[:128], Y_UP)
    far_a_1 = hop(down[128:256], Y_DOWN)
    far_b = hop(rows(up[384:512], down[384:512], token), X_SWAP)
    *sums, _ = particle_terms(1, fill[1], *shared, [up, down, b_side], sums)
    keep, send, grads = particle_terms(2, fill[2], *shared, [far_b, far_a_0, far_a_1], sums, core)
    return reduce_all(core, keep, send, grads, perm)


def solution(mesh):
    return jax.shard_map(
        local,
        mesh=mesh,
        in_specs=(
            P("dom", None, "pix"),
            P("dom", None, None, "pix"),
            P("dom", None),
            P("dom"),
            P("dom"),
            P("dom"),
            P(),
        ),
        out_specs=(P(), P("dom")),
        check_vma=False,
    )
```

```python
import functools
import math

import jax
import jax.numpy as jnp
from jax import lax
from jax.experimental import pallas as pl
from jax.experimental.pallas import tpu as pltpu
from jax.sharding import PartitionSpec as P

BOX = 256
GROUPS = 64
ZERN = 12
PAIRS = ZERN * (ZERN + 1) // 2
PHASE_GAIN = 40.0
RIDGE = 1.0

WIDE = 256
MOMENTS = 96
RIGHT_AT = 80

SIN_POLY = (3.141592580044675, -5.167706878922935, 2.5500313772212047, -0.5980451737557255, 0.07722012821305138)
COS_POLY = (0.9999999534415752, -4.934792857330457, 4.058411894717311, -1.3318800570964462, 0.2196966127309024)

X_SWAP = [(d, d ^ 1) for d in range(8)]
Y_UP = [(d, (d + 2) % 8) for d in range(8)]
Y_DOWN = [(d, (d - 2) % 8) for d in range(8)]
CORE_SWAP = [(p, p ^ 1) for p in range(32)]
CORE_GROUPS = [[2 * m + c for m in range(16)] for c in range(2)]

F32 = jnp.float32
BF16 = jnp.bfloat16
SMEM = pl.BlockSpec(memory_space=pltpu.SMEM)
VMEM = pl.BlockSpec(memory_space=pltpu.VMEM)


def params():
    return pltpu.CompilerParams(vmem_limit_bytes=16 * 1024 * 1024)


def horner(coeffs, z):
    acc = jnp.full_like(z, coeffs[-1])
    for c in coeffs[-2::-1]:
        acc = acc * z + c
    return acc


STAGES = [(0, 4), (4, 7), (7, 8)]
NT = (((1,), (1,)), ((), ()))


def sort_kernel(place, slot_class, class_ref, pose_ref, group_ref, defocus_ref, image_ref, *refs):
    sorted_ref, perm_ref, col_ref, row_ref, count_ref, perm = refs
    parts = perm.shape[0]

    @pl.when(pl.program_id(0) == 0)
    def _():
        y0 = place[0] >> 1
        x0 = place[0] & 1
        cls = class_ref[...]
        block = jnp.zeros_like(cls)
        for slot in range(8):
            up = ((slot >> 1) - y0) & 3
            side = (slot & 1) ^ x0
            near = jnp.where(up == 3, 2, 3) + 2 * side
            at = jnp.where(up == 0, side, jnp.where(up == 2, 6 + side, near))
            block = jnp.where(cls == slot_class[slot], at, block)
        key = lax.broadcasted_iota(jnp.int32, (8, parts), 0)
        hot = jnp.where(key == block, 1.0, 0.0)
        sub = lax.broadcasted_iota(jnp.int32, (parts, parts), 0)
        lane = lax.broadcasted_iota(jnp.int32, (parts, parts), 1)
        perm[...] = jnp.where(sub < lane, 1.0, 0.0).astype(BF16)
        before = jnp.dot(hot.astype(BF16), perm[...], preferred_element_type=F32)
        total = jnp.sum(hot, axis=1, keepdims=True)
        rank = jnp.zeros((1, parts), F32)
        start = jnp.zeros((1, 1), F32)
        for k in range(8):
            rank = rank + hot[k : k + 1] * (before[k : k + 1] + start)
            start = start + total[k : k + 1]
        perm[...] = jnp.where(sub == rank.astype(jnp.int32), 1.0, 0.0).astype(BF16)
        perm_ref[...] = perm[...]
        mark = lax.broadcasted_iota(jnp.int32, (16, parts), 0)
        rows = jnp.where(mark == 0, block.astype(F32), 0.0)
        rows = jnp.where(mark == 1, pose_ref[...].astype(F32), rows)
        rows = jnp.where(mark == 2, defocus_ref[...], rows)
        rows = jnp.where(mark == 3, group_ref[...].astype(F32), rows).astype(BF16)
        col_ref[...] = lax.dot_general(perm[...], rows, NT, preferred_element_type=F32)
        row_ref[...] = lax.dot_general(rows, perm[...], NT, preferred_element_type=F32)
        for k in range(9):
            count_ref[k] = jnp.sum(jnp.where(block < k, 1.0, 0.0)).astype(jnp.int32)

    sorted_ref[...] = jnp.dot(perm[...], image_ref[...], preferred_element_type=F32).astype(BF16)


def sort_particles(place, slot_class, class_row, pose_row, group_row, defocus_row, images):
    parts, cols = images.shape
    row = pl.BlockSpec((1, parts), lambda i: (0, 0))
    return pl.pallas_call(
        sort_kernel,
        grid=(cols // 512,),
        in_specs=[SMEM, SMEM, row, row, row, row, pl.BlockSpec((parts, 512), lambda i: (0, i))],
        out_specs=[
            pl.BlockSpec((parts, 512), lambda i: (0, i)),
            pl.BlockSpec((parts, parts), lambda i: (0, 0)),
            pl.BlockSpec((parts, 16), lambda i: (0, 0)),
            pl.BlockSpec((16, parts), lambda i: (0, 0)),
            SMEM,
        ],
        out_shape=[
            pltpu.HBM((parts, cols), BF16),
            pltpu.HBM((parts, parts), BF16),
            jax.ShapeDtypeStruct((parts, 16), F32),
            jax.ShapeDtypeStruct((16, parts), F32),
            jax.ShapeDtypeStruct((9,), jnp.int32),
        ],
        scratch_shapes=[pltpu.VMEM((parts, parts), BF16)],
        compiler_params=params(),
        cost_estimate=pl.CostEstimate(
            flops=2 * parts * parts * cols, bytes_accessed=4 * parts * cols, transcendentals=0
        ),
        name="sort_particles",
    )(place, slot_class, class_row, pose_row, group_row, defocus_row, images)


def pixel_grid(first, count):
    index = first + lax.broadcasted_iota(jnp.int32, (1, count), 1)
    scale = math.sqrt(2.0) / BOX
    freq_x = (index & (BOX // 2 - 1)).astype(F32) * scale
    freq_y = ((index >> 7) - BOX // 2).astype(F32) * scale
    return freq_x, freq_y


def zernike_rows(freq_x, freq_y):
    q = freq_x * freq_x + freq_y * freq_y
    re1, im1 = freq_x, freq_y
    re2 = freq_x * freq_x - freq_y * freq_y
    im2 = 2.0 * freq_x * freq_y
    re3 = re2 * re1 - im2 * im1
    im3 = re2 * im1 + im2 * re1
    re5 = re3 * re2 - im3 * im2
    im5 = re3 * im2 + im3 * re2
    r3 = 3.0 * q - 2.0
    r5 = 10.0 * q * q - 12.0 * q + 3.0
    ro = 5.0 * q - 4.0
    return [re1, im1, r3 * re1, r3 * im1, r5 * re1, r5 * im1, re3, im3, ro * re3, ro * im3, re5, im5]


def tile_edges(stage, parts):
    return [(0, 256, 512, 768), (256, 416, 672, 928, parts), (832, parts)][stage]


def terms_kernel(stage, fill, refs):
    late = stage == 2
    refs = list(refs)
    core = refs.pop(0) if late else None
    first, counts, col_ref, row_ref = refs[:4]
    refs = refs[4:]
    if stage > 0:
        old_moments, old_grads = refs[:2]
        refs = refs[2:]
    image_ref = refs.pop(0)
    refs, work = refs[:-7], refs[-7:]
    table, image, sums, basis, pairs, table_sem, image_sem = work
    if late:
        keep_ref, send_ref, grad_ref, moment_ref, full = refs[-5:]
        pieces = refs[:-5]
    else:
        moment_ref, grad_ref, token_ref = refs[-3:]
        pieces = refs[:-3]
        token_ref[...] = jnp.zeros_like(token_ref)
    parts = col_ref.shape[0]
    pix_count = image_ref.shape[1] // 2
    kb_from, kb_to = STAGES[stage]
    edges = tile_edges(stage, parts)
    row_from, row_to = edges[0], edges[-1]

    loads = []
    for i, (piece, src, src_col, dst, dst_col, rows, width) in enumerate(fill):
        loads.append(
            pltpu.make_async_copy(
                pieces[piece].at[pl.ds(src, rows), pl.ds(src_col, width)],
                table.at[pl.ds(dst, rows), pl.ds(dst_col, width)],
                table_sem.at[i],
            )
        )
    loads.append(
        pltpu.make_async_copy(image_ref.at[pl.ds(row_from, row_to - row_from), :], image, image_sem.at[0])
    )
    for copy in loads:
        copy.start()
    grad_ref[...] = old_grads[...] if stage > 0 else jnp.zeros_like(grad_ref)
    sums[...] = jnp.zeros_like(sums)
    freq_x, freq_y = pixel_grid(first[0], pix_count)
    q = freq_x * freq_x + freq_y * freq_y

    def lanes(v):
        return sum(v[:, 128 * i : 128 * i + 128] for i in range(v.shape[1] // 128))

    def work_on(at, rows):
        here = slice(at, at + rows)
        there = slice(at - row_from, at - row_from + rows)
        row = (col_ref[here, 0:1] * 256.0 + col_ref[here, 1:2]).astype(jnp.int32) - 256 * kb_from
        col = lax.broadcasted_iota(jnp.int32, (rows, 256 * (kb_to - kb_from)), 1)
        hot = jnp.where(col == row, 1.0, 0.0).astype(BF16)
        defocus = col_ref[here, 2:3] * (PHASE_GAIN / (2.0 * math.pi))
        group_hot = jnp.where(
            lax.broadcasted_iota(jnp.int32, (GROUPS, rows), 0) == row_ref[3:4, here].astype(jnp.int32), 1.0, 0.0
        ).astype(BF16)
        grad_sum = 0.0
        curv_sum = 0.0
        for pix in range(0, pix_count, WIDE):
            cols = slice(pix, pix + WIDE)
            other = slice(pix_count + pix, pix_count + pix + WIDE)
            proj_re = jnp.dot(hot, table[:, cols], preferred_element_type=F32)
            proj_im = jnp.dot(hot, table[:, other], preferred_element_type=F32)
            image_re = image[there, cols].astype(F32)
            image_im = image[there, other].astype(F32)
            q_sub = q[:, cols]

            turns = defocus * q_sub
            rest_turn = turns - jnp.floor(turns + 0.5)
            z = rest_turn * rest_turn
            s = rest_turn * horner(SIN_POLY, z)
            c = horner(COS_POLY, z)
            s2 = s + s
            sin_phi = s2 * c
            cos_phi = 1.0 - s2 * s

            power = proj_re * proj_re + proj_im * proj_im
            along = proj_re * image_re + proj_im * image_im
            across = proj_im * image_re - proj_re * image_im
            weight = (PHASE_GAIN * q_sub) * cos_phi
            sp = sin_phi * power
            grad_sum += lanes(weight * (sp + along))
            curv_sum += lanes(weight * weight * power)
            pred_power = sin_phi * sp
            cross = sin_phi * across

            cross_hi = cross.astype(BF16)
            cross_lo = (cross - cross_hi.astype(F32)).astype(BF16)
            sums[:, cols] += jnp.dot(group_hot, pred_power.astype(BF16), preferred_element_type=F32)
            sums[:, other] += jnp.dot(group_hot, cross_hi, preferred_element_type=F32) + jnp.dot(
                group_hot, cross_lo, preferred_element_type=F32
            )
        grad_ref[0:1, here] += jnp.sum(grad_sum.T, axis=0, keepdims=True)
        grad_ref[1:2, here] += jnp.sum(curv_sum.T, axis=0, keepdims=True)

    basis[...] = jnp.zeros_like(basis)
    for j, row in enumerate(zernike_rows(freq_x, freq_y)):
        basis[j : j + 1, :] = row
    pairs[72:80, :] = jnp.zeros((8, pix_count), F32)
    at = 0
    for j in range(ZERN):
        pairs[at : at + ZERN - j, :] = basis[j : j + 1, :] * basis[j:ZERN, :]
        at += ZERN - j

    for copy in loads:
        copy.wait()
    for at, end in zip(edges[:-1], edges[1:]):
        some = (counts[kb_from] < end) & (counts[kb_to] > at)
        pl.when(some)(functools.partial(work_on, at, end - at))

    normal = lax.dot_general(
        pairs[...], sums[:, :pix_count], NT, precision=lax.Precision.HIGHEST, preferred_element_type=F32
    )
    right = lax.dot_general(
        basis[...], sums[:, pix_count:], NT, precision=lax.Precision.HIGHEST, preferred_element_type=F32
    )
    if stage > 0:
        normal = normal + old_moments[0:RIGHT_AT, :]
        right = right + old_moments[RIGHT_AT:, :]
    moment_ref[0:RIGHT_AT, :] = normal
    moment_ref[RIGHT_AT:, :] = right

    if late:
        moments = moment_ref[...]
        full[...] = jnp.concatenate([moments[: MOMENTS // 2], moments[MOMENTS // 2 :]], axis=1)
        keep_ref[...] = full[pl.ds(pl.multiple_of(core[0] * 24, 8), 24), :]
        send_ref[...] = full[pl.ds(pl.multiple_of((1 - core[0]) * 24, 8), 24), :]


def particle_terms(stage, fill, first, counts, mark_cols, mark_rows, images, pieces, before=(), core=None):
    parts = mark_cols.shape[0]
    pix_count = images.shape[1] // 2
    late = stage == 2
    operands = [first, counts, mark_cols, mark_rows, *before]
    specs = [SMEM, SMEM] + [VMEM] * (2 + len(before))
    if late:
        operands = [core] + operands
        specs = [SMEM] + specs
    operands += [images, *pieces]
    specs += [pl.BlockSpec(memory_space=pltpu.HBM)] + [pl.BlockSpec(memory_space=pl.ANY)] * len(pieces)
    moments = jax.ShapeDtypeStruct((MOMENTS, GROUPS), F32)
    grads = jax.ShapeDtypeStruct((2, parts), F32)
    half = jax.ShapeDtypeStruct((24, 128), F32)
    kb_from, kb_to = STAGES[stage]
    edges = tile_edges(stage, parts)
    row_from, row_to = edges[0], edges[-1]
    work = [
        pltpu.VMEM((256 * (kb_to - kb_from), 2 * pix_count), BF16),
        pltpu.VMEM((row_to - row_from, 2 * pix_count), BF16),
        pltpu.VMEM((GROUPS, 2 * pix_count), F32),
        pltpu.VMEM((16, pix_count), F32),
        pltpu.VMEM((RIGHT_AT, pix_count), F32),
        pltpu.SemaphoreType.DMA((len(fill),)),
        pltpu.SemaphoreType.DMA((1,)),
    ]
    if late:
        out_shape = [half, half, grads]
        scratch = [pltpu.VMEM(moments.shape, F32), pltpu.VMEM((48, 128), F32)] + work
    else:
        out_shape = [moments, grads, jax.ShapeDtypeStruct((16, pix_count), BF16)]
        scratch = work

    def body(*refs):
        terms_kernel(stage, fill, refs)

    return pl.pallas_call(
        body,
        in_specs=specs,
        out_specs=[VMEM] * len(out_shape),
        out_shape=out_shape,
        scratch_shapes=scratch,
        compiler_params=params(),
        cost_estimate=pl.CostEstimate(
            flops=[4, 3, 1][stage] * 2 * parts * 2048 * pix_count,
            bytes_accessed=8 * 1024 * 1024,
            transcendentals=0,
        ),
        name="terms_%d" % stage,
    )(*operands)


def unsort_kernel(core, grad_ref, perm_ref, keep_ref, send_ref, split, full, perm, perm_sem):
    perm_load = pltpu.make_async_copy(perm_ref, perm, perm_sem.at[0])
    perm_load.start()
    rest = grad_ref[...]
    split[...] = jnp.zeros_like(split)
    for k in range(3):
        term = rest.astype(BF16).astype(F32)
        split[2 * k : 2 * k + 2, :] = term
        rest = rest - term
    perm_load.wait()
    back = jnp.dot(split[...].astype(BF16), perm[...], preferred_element_type=F32)
    grads = back[0:2] + back[2:4] + back[4:6]
    for h in range(2):
        for r in range(4):
            at = 512 * h + 128 * r
            full[8 * h + r : 8 * h + r + 1, :] = grads[0:1, at : at + 128]
            full[8 * h + 4 + r : 8 * h + 5 + r, :] = grads[1:2, at : at + 128]
    keep_ref[...] = full[pl.ds(pl.multiple_of(core[0] * 8, 8), 8), :]
    send_ref[...] = full[pl.ds(pl.multiple_of((1 - core[0]) * 8, 8), 8), :]


def unsort(core, grads, perm):
    half = jax.ShapeDtypeStruct((8, 128), F32)
    return pl.pallas_call(
        unsort_kernel,
        in_specs=[SMEM, VMEM, pl.BlockSpec(memory_space=pltpu.HBM)],
        out_shape=[half, half],
        scratch_shapes=[
            pltpu.VMEM((16, perm.shape[0]), F32),
            pltpu.VMEM((16, 128), F32),
            pltpu.VMEM(perm.shape, BF16),
            pltpu.SemaphoreType.DMA((1,)),
        ],
        compiler_params=params(),
        name="unsort",
    )(core, grads, perm)


def whiten_kernel(core, own_ref, other_ref, white_ref, score_ref, both, rows, sem):
    loads = [
        pltpu.make_async_copy(ref, both.at[pl.ds(pl.multiple_of(at * 32, 32), 32), :], sem.at[i])
        for i, (ref, at) in enumerate([(own_ref, core[0]), (other_ref, 1 - core[0])])
    ]
    for copy in loads:
        copy.start()
    for copy in loads:
        copy.wait()
    low = jnp.concatenate([both[0:24, :], both[32:56, :]], axis=0)
    moments = jnp.concatenate([low[:, :GROUPS], low[:, GROUPS:]], axis=0)
    at = 0
    rows[...] = jnp.zeros_like(rows)
    for j in range(ZERN):
        rows[j, j:ZERN, :] = moments[at : at + ZERN - j]
        at += ZERN - j
    right = moments[RIGHT_AT : RIGHT_AT + 16]
    line = [rows[j] for j in range(ZERN)]
    lane_row = lax.broadcasted_iota(jnp.int32, (16, GROUPS), 0)
    done = jnp.zeros((16, GROUPS), F32)
    for j in range(ZERN):
        inv = lax.rsqrt(line[j][j : j + 1] + RIDGE)
        col = line[j] * inv
        value = right[j : j + 1] * inv
        done = jnp.where(lane_row == j, value, done)
        right = right - col * value
        for i in range(j + 1, ZERN):
            line[i] = line[i] - col[i : i + 1] * col
    white_ref[...] = done[:ZERN]
    for h in range(2):
        grad = both[32 * h + 24 : 32 * h + 28, :]
        curv = both[32 * h + 28 : 32 * h + 32, :]
        score_ref[4 * h : 4 * h + 4, :] = -grad * lax.rsqrt(curv + 1e-06)


def spread(block, count):
    return jnp.broadcast_to(block[None], (count,) + block.shape)


def reduce_all(core, keep, send, grads, perm):
    mine = keep + lax.ppermute(send, "pix", CORE_SWAP)
    moments = jnp.sum(lax.all_to_all(spread(mine, 8), "dom", 0, 0), axis=0)
    keep, send = unsort(core, grads, perm)
    grads = keep + lax.ppermute(send, "pix", CORE_SWAP)
    mine = jnp.concatenate([moments, grads], axis=0)
    mine = jnp.sum(lax.all_to_all(spread(mine, 16), "pix", 0, 0, axis_index_groups=CORE_GROUPS), axis=0)
    other = lax.ppermute(mine, "pix", CORE_SWAP)
    white, score = pl.pallas_call(
        whiten_kernel,
        in_specs=[SMEM] + [pl.BlockSpec(memory_space=pl.ANY)] * 2,
        out_shape=[
            jax.ShapeDtypeStruct((ZERN, GROUPS), F32),
            jax.ShapeDtypeStruct((8, 128), F32),
        ],
        scratch_shapes=[
            pltpu.VMEM((64, 128), F32),
            pltpu.VMEM((ZERN, 16, GROUPS), F32),
            pltpu.SemaphoreType.DMA((2,)),
        ],
        compiler_params=params(),
        name="whiten",
    )(core, mine, other)
    return white.T, score.reshape(-1)


def hop(block, perm):
    return lax.ppermute(block, "dom", perm)


def fills(pix_count):
    half = pix_count // 2

    def parted(piece, src, dst, rows, at):
        return [(piece, src, part * half, dst, part * pix_count + at, rows, half) for part in range(2)]

    own = [(piece, 0, 0, 256 * piece, 0, 256, 2 * pix_count) for piece in range(4)]
    next_a = parted(0, 0, 0, 256, 0) + parted(1, 0, 256, 256, 0)
    next_b = parted(2, 0, 0, 512, half)
    far = parted(0, 256, 512, 128, 0) + parted(1, 256, 640, 128, 0)
    far += parted(0, 384, 512, 128, half) + parted(1, 384, 640, 128, half)
    last = parted(0, 0, 0, 256, half) + parted(1, 0, 0, 128, 0) + parted(2, 0, 128, 128, 0)
    return [own, next_a + next_b + far, last]


def local(images, slices, class_of, pose_of, group_of, defocus, slot_class):
    parts, _, pix_count = images.shape
    poses = slices.shape[1]
    dom_at = lax.axis_index("dom").astype(jnp.int32).reshape(1)
    pix_at = lax.axis_index("pix").astype(jnp.int32)
    core = (pix_at & 1).reshape(1)
    first = (pix_at * pix_count).reshape(1)
    half = pix_count // 2
    flat = slices.reshape(poses, 2 * pix_count)

    def rows(*blocks):
        return jnp.concatenate(blocks, axis=0)

    def cols(*blocks):
        return jnp.concatenate(blocks, axis=1)

    def part_a(block):
        return cols(block[:, :half], block[:, pix_count : pix_count + half])

    def part_b(block):
        return cols(block[:, half:pix_count], block[:, pix_count + half :])

    side = hop(flat, X_SWAP)
    below = hop(flat, Y_UP)
    above = hop(flat, Y_DOWN)
    image_rows, perm, mark_cols, mark_rows, counts = sort_particles(
        dom_at,
        slot_class,
        class_of.reshape(1, parts),
        pose_of[None, :],
        group_of[None, :],
        defocus.astype(F32)[None, :],
        images.reshape(parts, 2 * pix_count),
    )

    up = hop(rows(part_a(side), part_a(below[:128]), part_b(below[:128])), Y_UP)
    down = hop(rows(part_a(side), part_a(above[128:]), part_b(above[128:]), image_rows[:16, :pix_count]), Y_DOWN)
    b_side = hop(rows(part_b(below), part_b(above)), X_SWAP)
    fill = fills(pix_count)
    shared = (first, counts, mark_cols, mark_rows, image_rows)
    *sums, token = particle_terms(0, fill[0], *shared, [flat, side, below, above])

    far_a_0 = hop(up[:128], Y_UP)
    far_a_1 = hop(down[128:256], Y_DOWN)
    far_b = hop(rows(up[384:512], down[384:512], token), X_SWAP)
    *sums, _ = particle_terms(1, fill[1], *shared, [up, down, b_side], sums)
    keep, send, grads = particle_terms(2, fill[2], *shared, [far_b, far_a_0, far_a_1], sums, core)
    return reduce_all(core, keep, send, grads, perm)


def solution(mesh):
    return jax.shard_map(
        local,
        mesh=mesh,
        in_specs=(
            P("dom", None, "pix"),
            P("dom", None, None, "pix"),
            P("dom", None),
            P("dom"),
            P("dom"),
            P("dom"),
            P(),
        ),
        out_specs=(P(), P("dom")),
        check_vma=False,
    )
```

```python
import functools
import math

import jax
import jax.numpy as jnp
import numpy as np
from jax import lax
from jax.experimental import pallas as pl
from jax.experimental.pallas import tpu as pltpu
from jax.sharding import PartitionSpec as P

BOX = 256
GROUPS = 64
ZERN = 12
PAIRS = ZERN * (ZERN + 1) // 2
PHASE_GAIN = 40.0
RIDGE = 1.0

WIDE = 256
MOMENTS = 48
RIGHT_AT = 36

SIN_POLY = (3.141592580044675, -5.167706878922935, 2.5500313772212047, -0.5980451737557255, 0.07722012821305138)
COS_POLY = (0.9999999534415752, -4.934792857330457, 4.058411894717311, -1.3318800570964462, 0.2196966127309024)

X_SWAP = [(d, d ^ 1) for d in range(8)]
Y_UP = [(d, (d + 2) % 8) for d in range(8)]
Y_DOWN = [(d, (d - 2) % 8) for d in range(8)]
CORE_SWAP = [(p, p ^ 1) for p in range(32)]
CORE_GROUPS = [[2 * m + c for m in range(16)] for c in range(2)]

F32 = jnp.float32
BF16 = jnp.bfloat16
SMEM = pl.BlockSpec(memory_space=pltpu.SMEM)
VMEM = pl.BlockSpec(memory_space=pltpu.VMEM)


def params():
    return pltpu.CompilerParams(vmem_limit_bytes=16 * 1024 * 1024)


def horner(coeffs, z):
    acc = jnp.full_like(z, coeffs[-1])
    for c in coeffs[-2::-1]:
        acc = acc * z + c
    return acc


STAGES = [(0, 4), (4, 7), (7, 8)]
NT = (((1,), (1,)), ((), ()))


def sort_kernel(place, slot_class, class_ref, pose_ref, group_ref, defocus_ref, image_ref, *refs):
    sorted_ref, perm_ref, col_ref, row_ref, count_ref, perm = refs
    parts = perm.shape[0]

    @pl.when(pl.program_id(0) == 0)
    def _():
        y0 = place[0] >> 1
        x0 = place[0] & 1
        cls = class_ref[...]
        block = jnp.zeros_like(cls)
        for slot in range(8):
            up = ((slot >> 1) - y0) & 3
            side = (slot & 1) ^ x0
            near = jnp.where(up == 3, 2, 3) + 2 * side
            at = jnp.where(up == 0, side, jnp.where(up == 2, 6 + side, near))
            block = jnp.where(cls == slot_class[slot], at, block)
        key = lax.broadcasted_iota(jnp.int32, (8, parts), 0)
        hot = jnp.where(key == block, 1.0, 0.0)
        sub = lax.broadcasted_iota(jnp.int32, (parts, parts), 0)
        lane = lax.broadcasted_iota(jnp.int32, (parts, parts), 1)
        perm[...] = jnp.where(sub < lane, 1.0, 0.0).astype(BF16)
        before = jnp.dot(hot.astype(BF16), perm[...], preferred_element_type=F32)
        total = jnp.sum(hot, axis=1, keepdims=True)
        rank = jnp.zeros((1, parts), F32)
        start = jnp.zeros((1, 1), F32)
        for k in range(8):
            rank = rank + hot[k : k + 1] * (before[k : k + 1] + start)
            start = start + total[k : k + 1]
        perm[...] = jnp.where(sub == rank.astype(jnp.int32), 1.0, 0.0).astype(BF16)
        perm_ref[...] = perm[...]
        mark = lax.broadcasted_iota(jnp.int32, (16, parts), 0)
        rows = jnp.where(mark == 0, block.astype(F32), 0.0)
        rows = jnp.where(mark == 1, pose_ref[...].astype(F32), rows)
        rows = jnp.where(mark == 2, defocus_ref[...], rows)
        rows = jnp.where(mark == 3, group_ref[...].astype(F32), rows).astype(BF16)
        col_ref[...] = lax.dot_general(perm[...], rows, NT, preferred_element_type=F32)
        row_ref[...] = lax.dot_general(rows, perm[...], NT, preferred_element_type=F32)
        for k in range(9):
            count_ref[k] = jnp.sum(jnp.where(block < k, 1.0, 0.0)).astype(jnp.int32)

    sorted_ref[...] = jnp.dot(perm[...], image_ref[...], preferred_element_type=F32).astype(BF16)


def sort_particles(place, slot_class, class_row, pose_row, group_row, defocus_row, images):
    parts, cols = images.shape
    row = pl.BlockSpec((1, parts), lambda i: (0, 0))
    return pl.pallas_call(
        sort_kernel,
        grid=(cols // 512,),
        in_specs=[SMEM, SMEM, row, row, row, row, pl.BlockSpec((parts, 512), lambda i: (0, i))],
        out_specs=[
            pl.BlockSpec((parts, 512), lambda i: (0, i)),
            pl.BlockSpec((parts, parts), lambda i: (0, 0)),
            pl.BlockSpec((parts, 16), lambda i: (0, 0)),
            pl.BlockSpec((16, parts), lambda i: (0, 0)),
            SMEM,
        ],
        out_shape=[
            pltpu.HBM((parts, cols), BF16),
            pltpu.HBM((parts, parts), BF16),
            jax.ShapeDtypeStruct((parts, 16), F32),
            jax.ShapeDtypeStruct((16, parts), F32),
            jax.ShapeDtypeStruct((9,), jnp.int32),
        ],
        scratch_shapes=[pltpu.VMEM((parts, parts), BF16)],
        compiler_params=params(),
        cost_estimate=pl.CostEstimate(
            flops=2 * parts * parts * cols, bytes_accessed=4 * parts * cols, transcendentals=0
        ),
        name="sort_particles",
    )(place, slot_class, class_row, pose_row, group_row, defocus_row, images)


def legendre(q, count):
    x = 2.0 * q - 1.0
    rows = [q * 0.0 + 1.0, x]
    for n in range(1, count - 1):
        rows.append(((2 * n + 1) * x * rows[n] - n * rows[n - 1]) / (n + 1))
    return rows[:count]


def product_rows(freq_x, freq_y):
    q = freq_x * freq_x + freq_y * freq_y
    polys = legendre(q, 5)
    rows = [q * p for p in polys]
    re2, im2 = freq_x * freq_x - freq_y * freq_y, 2.0 * freq_x * freq_y
    re, im = re2, im2
    for count in (5, 4, 3, 2, 1):
        for p in polys[:count]:
            rows += [re * p, im * p]
        re, im = re * re2 - im * im2, re * im2 + im * re2
    return rows


def product_weights():
    angle = np.arange(24) * (2.0 * np.pi / 24) + 0.1
    radius = np.sqrt((np.cos((np.arange(8) + 0.5) * (np.pi / 8)) + 1.0) / 2.0)
    x = (radius[:, None] * np.cos(angle)).reshape(-1)
    y = (radius[:, None] * np.sin(angle)).reshape(-1)
    zern = zernike_rows(x, y)
    pairs = np.stack([zern[j] * zern[k] for j in range(ZERN) for k in range(j, ZERN)], axis=1)
    rows = np.stack(product_rows(x, y), axis=1)
    weights = np.linalg.lstsq(rows, pairs, rcond=None)[0].T
    weights = np.where(np.abs(weights) < 1e-10, 0.0, np.round(weights, 12))
    out = np.zeros((80, RIGHT_AT + 4))
    out[:PAIRS, : rows.shape[1]] = weights
    return out.astype(np.float32)


def pixel_grid(first, count):
    index = first + lax.broadcasted_iota(jnp.int32, (1, count), 1)
    scale = math.sqrt(2.0) / BOX
    freq_x = (index & (BOX // 2 - 1)).astype(F32) * scale
    freq_y = ((index >> 7) - BOX // 2).astype(F32) * scale
    return freq_x, freq_y


def zernike_rows(freq_x, freq_y):
    q = freq_x * freq_x + freq_y * freq_y
    re1, im1 = freq_x, freq_y
    re2 = freq_x * freq_x - freq_y * freq_y
    im2 = 2.0 * freq_x * freq_y
    re3 = re2 * re1 - im2 * im1
    im3 = re2 * im1 + im2 * re1
    re5 = re3 * re2 - im3 * im2
    im5 = re3 * im2 + im3 * re2
    r3 = 3.0 * q - 2.0
    r5 = 10.0 * q * q - 12.0 * q + 3.0
    ro = 5.0 * q - 4.0
    return [re1, im1, r3 * re1, r3 * im1, r5 * re1, r5 * im1, re3, im3, ro * re3, ro * im3, re5, im5]


def tile_edges(stage, parts):
    return [(0, 256, 512, 768), (256, 416, 672, 928, parts), (832, parts)][stage]


def terms_kernel(stage, fill, refs):
    late = stage == 2
    refs = list(refs)
    core = refs.pop(0) if late else None
    first, counts, col_ref, row_ref = refs[:4]
    refs = refs[4:]
    if stage > 0:
        old_moments, old_grads = refs[:2]
        refs = refs[2:]
    image_ref = refs.pop(0)
    refs, work = refs[:-7], refs[-7:]
    table, image, sums, basis, products, table_sem, image_sem = work
    if late:
        keep_ref, send_ref, grad_ref, moment_ref, full = refs[-5:]
        pieces = refs[:-5]
    else:
        moment_ref, grad_ref, token_ref = refs[-3:]
        pieces = refs[:-3]
        token_ref[...] = jnp.zeros_like(token_ref)
    parts = col_ref.shape[0]
    pix_count = image_ref.shape[1] // 2
    kb_from, kb_to = STAGES[stage]
    edges = tile_edges(stage, parts)
    row_from, row_to = edges[0], edges[-1]

    loads = []
    for i, (piece, src, src_col, dst, dst_col, rows, width) in enumerate(fill):
        loads.append(
            pltpu.make_async_copy(
                pieces[piece].at[pl.ds(src, rows), pl.ds(src_col, width)],
                table.at[pl.ds(dst, rows), pl.ds(dst_col, width)],
                table_sem.at[i],
            )
        )
    loads.append(
        pltpu.make_async_copy(image_ref.at[pl.ds(row_from, row_to - row_from), :], image, image_sem.at[0])
    )
    for copy in loads:
        copy.start()
    grad_ref[...] = old_grads[...] if stage > 0 else jnp.zeros_like(grad_ref)
    sums[...] = jnp.zeros_like(sums)
    freq_x, freq_y = pixel_grid(first[0], pix_count)
    q = freq_x * freq_x + freq_y * freq_y

    def lanes(v):
        return sum(v[:, 128 * i : 128 * i + 128] for i in range(v.shape[1] // 128))

    def work_on(at, rows):
        here = slice(at, at + rows)
        there = slice(at - row_from, at - row_from + rows)
        row = (col_ref[here, 0:1] * 256.0 + col_ref[here, 1:2]).astype(jnp.int32) - 256 * kb_from
        col = lax.broadcasted_iota(jnp.int32, (rows, 256 * (kb_to - kb_from)), 1)
        hot = jnp.where(col == row, 1.0, 0.0).astype(BF16)
        defocus = col_ref[here, 2:3] * (PHASE_GAIN / (2.0 * math.pi))
        group_hot = jnp.where(
            lax.broadcasted_iota(jnp.int32, (GROUPS, rows), 0) == row_ref[3:4, here].astype(jnp.int32), 1.0, 0.0
        ).astype(BF16)
        grad_sum = 0.0
        curv_sum = 0.0
        for pix in range(0, pix_count, WIDE):
            cols = slice(pix, pix + WIDE)
            other = slice(pix_count + pix, pix_count + pix + WIDE)
            proj_re = jnp.dot(hot, table[:, cols], preferred_element_type=F32)
            proj_im = jnp.dot(hot, table[:, other], preferred_element_type=F32)
            image_re = image[there, cols].astype(F32)
            image_im = image[there, other].astype(F32)
            q_sub = q[:, cols]

            turns = defocus * q_sub
            rest_turn = turns - jnp.floor(turns + 0.5)
            z = rest_turn * rest_turn
            s = rest_turn * horner(SIN_POLY, z)
            c = horner(COS_POLY, z)
            s2 = s + s
            sin_phi = s2 * c
            cos_phi = 1.0 - s2 * s

            power = proj_re * proj_re + proj_im * proj_im
            along = proj_re * image_re + proj_im * image_im
            across = proj_im * image_re - proj_re * image_im
            weight = (PHASE_GAIN * q_sub) * cos_phi
            sp = sin_phi * power
            grad_sum += lanes(weight * (sp + along))
            curv_sum += lanes(weight * weight * power)
            pred_power = sin_phi * sp
            cross = sin_phi * across

            cross_hi = cross.astype(BF16)
            cross_lo = (cross - cross_hi.astype(F32)).astype(BF16)
            sums[:, cols] += jnp.dot(group_hot, pred_power.astype(BF16), preferred_element_type=F32)
            sums[:, other] += jnp.dot(group_hot, cross_hi, preferred_element_type=F32) + jnp.dot(
                group_hot, cross_lo, preferred_element_type=F32
            )
        grad_ref[0:1, here] += jnp.sum(grad_sum.T, axis=0, keepdims=True)
        grad_ref[1:2, here] += jnp.sum(curv_sum.T, axis=0, keepdims=True)

    products[...] = jnp.zeros_like(products)
    for j, row in enumerate(product_rows(freq_x, freq_y)):
        products[j : j + 1, :] = row
    basis[...] = jnp.zeros_like(basis)
    for j, row in enumerate(zernike_rows(freq_x, freq_y)):
        basis[j : j + 1, :] = row

    for copy in loads:
        copy.wait()
    for at, end in zip(edges[:-1], edges[1:]):
        some = (counts[kb_from] < end) & (counts[kb_to] > at)
        pl.when(some)(functools.partial(work_on, at, end - at))

    normal = lax.dot_general(
        products[...], sums[:, :pix_count], NT, precision=lax.Precision.HIGHEST, preferred_element_type=F32
    )
    right = lax.dot_general(
        basis[...], sums[:, pix_count:], NT, precision=lax.Precision.HIGHEST, preferred_element_type=F32
    )
    moments = jnp.concatenate([normal[:RIGHT_AT], right[:ZERN]], axis=0)
    if stage > 0:
        moments = moments + old_moments[...]
    moment_ref[...] = moments

    if late:
        half = MOMENTS // 2
        full[...] = jnp.zeros_like(full)
        packed = jnp.concatenate([moments[:half], moments[half:]], axis=1)
        full[0:12] = packed[0:12]
        full[16:28] = packed[12:24]
        keep_ref[...] = full[pl.ds(pl.multiple_of(core[0] * 16, 16), 16), :]
        send_ref[...] = full[pl.ds(pl.multiple_of((1 - core[0]) * 16, 16), 16), :]


def particle_terms(stage, fill, first, counts, mark_cols, mark_rows, images, pieces, before=(), core=None):
    parts = mark_cols.shape[0]
    pix_count = images.shape[1] // 2
    late = stage == 2
    operands = [first, counts, mark_cols, mark_rows, *before]
    specs = [SMEM, SMEM] + [VMEM] * (2 + len(before))
    if late:
        operands = [core] + operands
        specs = [SMEM] + specs
    operands += [images, *pieces]
    specs += [pl.BlockSpec(memory_space=pltpu.HBM)] + [pl.BlockSpec(memory_space=pl.ANY)] * len(pieces)
    moments = jax.ShapeDtypeStruct((MOMENTS, GROUPS), F32)
    grads = jax.ShapeDtypeStruct((2, parts), F32)
    half = jax.ShapeDtypeStruct((16, 128), F32)
    kb_from, kb_to = STAGES[stage]
    edges = tile_edges(stage, parts)
    row_from, row_to = edges[0], edges[-1]
    work = [
        pltpu.VMEM((256 * (kb_to - kb_from), 2 * pix_count), BF16),
        pltpu.VMEM((row_to - row_from, 2 * pix_count), BF16),
        pltpu.VMEM((GROUPS, 2 * pix_count), F32),
        pltpu.VMEM((16, pix_count), F32),
        pltpu.VMEM((RIGHT_AT + 4, pix_count), F32),
        pltpu.SemaphoreType.DMA((len(fill),)),
        pltpu.SemaphoreType.DMA((1,)),
    ]
    if late:
        out_shape = [half, half, grads]
        scratch = [pltpu.VMEM(moments.shape, F32), pltpu.VMEM((32, 128), F32)] + work
    else:
        out_shape = [moments, grads, jax.ShapeDtypeStruct((16, pix_count), BF16)]
        scratch = work

    def body(*refs):
        terms_kernel(stage, fill, refs)

    return pl.pallas_call(
        body,
        in_specs=specs,
        out_specs=[VMEM] * len(out_shape),
        out_shape=out_shape,
        scratch_shapes=scratch,
        compiler_params=params(),
        cost_estimate=pl.CostEstimate(
            flops=[4, 3, 1][stage] * 2 * parts * 2048 * pix_count,
            bytes_accessed=8 * 1024 * 1024,
            transcendentals=0,
        ),
        name="terms_%d" % stage,
    )(*operands)


def unsort_kernel(core, grad_ref, perm_ref, keep_ref, send_ref, split, full, perm, perm_sem):
    perm_load = pltpu.make_async_copy(perm_ref, perm, perm_sem.at[0])
    perm_load.start()
    rest = grad_ref[...]
    split[...] = jnp.zeros_like(split)
    for k in range(3):
        term = rest.astype(BF16).astype(F32)
        split[2 * k : 2 * k + 2, :] = term
        rest = rest - term
    perm_load.wait()
    back = jnp.dot(split[...].astype(BF16), perm[...], preferred_element_type=F32)
    grads = back[0:2] + back[2:4] + back[4:6]
    for h in range(2):
        for r in range(4):
            at = 512 * h + 128 * r
            full[8 * h + r : 8 * h + r + 1, :] = grads[0:1, at : at + 128]
            full[8 * h + 4 + r : 8 * h + 5 + r, :] = grads[1:2, at : at + 128]
    keep_ref[...] = full[pl.ds(pl.multiple_of(core[0] * 8, 8), 8), :]
    send_ref[...] = full[pl.ds(pl.multiple_of((1 - core[0]) * 8, 8), 8), :]


def unsort(core, grads, perm):
    half = jax.ShapeDtypeStruct((8, 128), F32)
    return pl.pallas_call(
        unsort_kernel,
        in_specs=[SMEM, VMEM, pl.BlockSpec(memory_space=pltpu.HBM)],
        out_shape=[half, half],
        scratch_shapes=[
            pltpu.VMEM((16, perm.shape[0]), F32),
            pltpu.VMEM((16, 128), F32),
            pltpu.VMEM(perm.shape, BF16),
            pltpu.SemaphoreType.DMA((1,)),
        ],
        compiler_params=params(),
        name="unsort",
    )(core, grads, perm)


def whiten_kernel(core, own_ref, other_ref, weight_ref, white_ref, score_ref, both, rows, sem):
    loads = [
        pltpu.make_async_copy(ref, both.at[pl.ds(pl.multiple_of(at * 24, 8), 24), :], sem.at[i])
        for i, (ref, at) in enumerate([(own_ref, core[0]), (other_ref, 1 - core[0])])
    ]
    for copy in loads:
        copy.start()
    for copy in loads:
        copy.wait()
    low = jnp.concatenate([both[0:12, :], both[24:36, :]], axis=0)
    moments = jnp.concatenate([low[:, :GROUPS], low[:, GROUPS:]], axis=0)
    right = jnp.concatenate([moments[RIGHT_AT:], jnp.zeros((4, GROUPS), F32)], axis=0)
    moments = jnp.dot(
        weight_ref[...], moments[: RIGHT_AT + 4], precision=lax.Precision.HIGHEST, preferred_element_type=F32
    )
    at = 0
    rows[...] = jnp.zeros_like(rows)
    for j in range(ZERN):
        rows[j, j:ZERN, :] = moments[at : at + ZERN - j]
        at += ZERN - j
    line = [rows[j] for j in range(ZERN)]
    lane_row = lax.broadcasted_iota(jnp.int32, (16, GROUPS), 0)
    done = jnp.zeros((16, GROUPS), F32)
    for j in range(ZERN):
        inv = lax.rsqrt(line[j][j : j + 1] + RIDGE)
        col = line[j] * inv
        value = right[j : j + 1] * inv
        done = jnp.where(lane_row == j, value, done)
        right = right - col * value
        for i in range(j + 1, ZERN):
            line[i] = line[i] - col[i : i + 1] * col
    white_ref[...] = done[:ZERN]
    for h in range(2):
        grad = both[24 * h + 16 : 24 * h + 20, :]
        curv = both[24 * h + 20 : 24 * h + 24, :]
        score_ref[4 * h : 4 * h + 4, :] = -grad * lax.rsqrt(curv + 1e-06)


def spread(block, count):
    return jnp.broadcast_to(block[None], (count,) + block.shape)


def reduce_all(core, keep, send, grads, perm):
    mine = keep + lax.ppermute(send, "pix", CORE_SWAP)
    moments = jnp.sum(lax.all_to_all(spread(mine, 8), "dom", 0, 0), axis=0)
    keep, send = unsort(core, grads, perm)
    grads = keep + lax.ppermute(send, "pix", CORE_SWAP)
    mine = jnp.concatenate([moments, grads], axis=0)
    mine = jnp.sum(lax.all_to_all(spread(mine, 16), "pix", 0, 0, axis_index_groups=CORE_GROUPS), axis=0)
    other = lax.ppermute(mine, "pix", CORE_SWAP)
    white, score = pl.pallas_call(
        whiten_kernel,
        in_specs=[SMEM] + [pl.BlockSpec(memory_space=pl.ANY)] * 2 + [VMEM],
        out_shape=[
            jax.ShapeDtypeStruct((ZERN, GROUPS), F32),
            jax.ShapeDtypeStruct((8, 128), F32),
        ],
        scratch_shapes=[
            pltpu.VMEM((48, 128), F32),
            pltpu.VMEM((ZERN, 16, GROUPS), F32),
            pltpu.SemaphoreType.DMA((2,)),
        ],
        compiler_params=params(),
        name="whiten",
    )(core, mine, other, jnp.asarray(product_weights()))
    return white.T, score.reshape(-1)


def hop(block, perm):
    return lax.ppermute(block, "dom", perm)


def fills(pix_count):
    half = pix_count // 2

    def parted(piece, src, dst, rows, at):
        return [(piece, src, part * half, dst, part * pix_count + at, rows, half) for part in range(2)]

    own = [(piece, 0, 0, 256 * piece, 0, 256, 2 * pix_count) for piece in range(4)]
    next_a = parted(0, 0, 0, 256, 0) + parted(1, 0, 256, 256, 0)
    next_b = parted(2, 0, 0, 512, half)
    far = parted(0, 256, 512, 128, 0) + parted(1, 256, 640, 128, 0)
    far += parted(0, 384, 512, 128, half) + parted(1, 384, 640, 128, half)
    last = parted(0, 0, 0, 256, half) + parted(1, 0, 0, 128, 0) + parted(2, 0, 128, 128, 0)
    return [own, next_a + next_b + far, last]


def local(images, slices, class_of, pose_of, group_of, defocus, slot_class):
    parts, _, pix_count = images.shape
    poses = slices.shape[1]
    dom_at = lax.axis_index("dom").astype(jnp.int32).reshape(1)
    pix_at = lax.axis_index("pix").astype(jnp.int32)
    core = (pix_at & 1).reshape(1)
    first = (pix_at * pix_count).reshape(1)
    half = pix_count // 2
    flat = slices.reshape(poses, 2 * pix_count)

    def rows(*blocks):
        return jnp.concatenate(blocks, axis=0)

    def cols(*blocks):
        return jnp.concatenate(blocks, axis=1)

    def part_a(block):
        return cols(block[:, :half], block[:, pix_count : pix_count + half])

    def part_b(block):
        return cols(block[:, half:pix_count], block[:, pix_count + half :])

    side = hop(flat, X_SWAP)
    below = hop(flat, Y_UP)
    above = hop(flat, Y_DOWN)
    image_rows, perm, mark_cols, mark_rows, counts = sort_particles(
        dom_at,
        slot_class,
        class_of.reshape(1, parts),
        pose_of[None, :],
        group_of[None, :],
        defocus.astype(F32)[None, :],
        images.reshape(parts, 2 * pix_count),
    )

    up = hop(rows(part_a(side), part_a(below[:128]), part_b(below[:128])), Y_UP)
    down = hop(rows(part_a(side), part_a(above[128:]), part_b(above[128:]), image_rows[:16, :pix_count]), Y_DOWN)
    b_side = hop(rows(part_b(below), part_b(above)), X_SWAP)
    fill = fills(pix_count)
    shared = (first, counts, mark_cols, mark_rows, image_rows)
    *sums, token = particle_terms(0, fill[0], *shared, [flat, side, below, above])

    far_a_0 = hop(up[:128], Y_UP)
    far_a_1 = hop(down[128:256], Y_DOWN)
    far_b = hop(rows(up[384:512], down[384:512], token), X_SWAP)
    *sums, _ = particle_terms(1, fill[1], *shared, [up, down, b_side], sums)
    keep, send, grads = particle_terms(2, fill[2], *shared, [far_b, far_a_0, far_a_1], sums, core)
    return reduce_all(core, keep, send, grads, perm)


def solution(mesh):
    return jax.shard_map(
        local,
        mesh=mesh,
        in_specs=(
            P("dom", None, "pix"),
            P("dom", None, None, "pix"),
            P("dom", None),
            P("dom"),
            P("dom"),
            P("dom"),
            P(),
        ),
        out_specs=(P(), P("dom")),
        check_vma=False,
    )
```

```python
import functools
import math

import jax
import jax.numpy as jnp
import numpy as np
from jax import lax
from jax.experimental import pallas as pl
from jax.experimental.pallas import tpu as pltpu
from jax.sharding import PartitionSpec as P

BOX = 256
GROUPS = 64
ZERN = 12
PAIRS = ZERN * (ZERN + 1) // 2
PHASE_GAIN = 40.0
RIDGE = 1.0

WIDE = 256
MOMENTS = 48
RIGHT_AT = 36

SIN_POLY = (3.141592580044675, -5.167706878922935, 2.5500313772212047, -0.5980451737557255, 0.07722012821305138)
COS_POLY = (0.9999999534415752, -4.934792857330457, 4.058411894717311, -1.3318800570964462, 0.2196966127309024)

X_SWAP = [(d, d ^ 1) for d in range(8)]
Y_UP = [(d, (d + 2) % 8) for d in range(8)]
Y_DOWN = [(d, (d - 2) % 8) for d in range(8)]
CORE_SWAP = [(p, p ^ 1) for p in range(32)]
CORE_GROUPS = [[2 * m + c for m in range(16)] for c in range(2)]

F32 = jnp.float32
BF16 = jnp.bfloat16
SMEM = pl.BlockSpec(memory_space=pltpu.SMEM)
VMEM = pl.BlockSpec(memory_space=pltpu.VMEM)


def params():
    return pltpu.CompilerParams(vmem_limit_bytes=16 * 1024 * 1024)


def horner(coeffs, z):
    acc = jnp.full_like(z, coeffs[-1])
    for c in coeffs[-2::-1]:
        acc = acc * z + c
    return acc


STAGES = [(0, 4), (4, 7), (7, 8)]
NT = (((1,), (1,)), ((), ()))


def sort_kernel(place, slot_class, class_ref, pose_ref, group_ref, defocus_ref, image_ref, *refs):
    sorted_ref, perm_ref, col_ref, row_ref, count_ref, perm = refs
    parts = perm.shape[0]

    @pl.when(pl.program_id(0) == 0)
    def _():
        y0 = place[0] >> 1
        x0 = place[0] & 1
        cls = class_ref[...]
        block = jnp.zeros_like(cls)
        for slot in range(8):
            up = ((slot >> 1) - y0) & 3
            side = (slot & 1) ^ x0
            near = jnp.where(up == 3, 2, 3) + 2 * side
            at = jnp.where(up == 0, side, jnp.where(up == 2, 6 + side, near))
            block = jnp.where(cls == slot_class[slot], at, block)
        key = lax.broadcasted_iota(jnp.int32, (8, parts), 0)
        hot = jnp.where(key == block, 1.0, 0.0)
        sub = lax.broadcasted_iota(jnp.int32, (parts, parts), 0)
        lane = lax.broadcasted_iota(jnp.int32, (parts, parts), 1)
        perm[...] = jnp.where(sub < lane, 1.0, 0.0).astype(BF16)
        before = jnp.dot(hot.astype(BF16), perm[...], preferred_element_type=F32)
        total = jnp.sum(hot, axis=1, keepdims=True)
        rank = jnp.zeros((1, parts), F32)
        start = jnp.zeros((1, 1), F32)
        for k in range(8):
            rank = rank + hot[k : k + 1] * (before[k : k + 1] + start)
            start = start + total[k : k + 1]
        perm[...] = jnp.where(sub == rank.astype(jnp.int32), 1.0, 0.0).astype(BF16)
        perm_ref[...] = perm[...]
        mark = lax.broadcasted_iota(jnp.int32, (16, parts), 0)
        rows = jnp.where(mark == 0, block.astype(F32), 0.0)
        rows = jnp.where(mark == 1, pose_ref[...].astype(F32), rows)
        rows = jnp.where(mark == 2, defocus_ref[...], rows)
        rows = jnp.where(mark == 3, group_ref[...].astype(F32), rows).astype(BF16)
        col_ref[...] = lax.dot_general(perm[...], rows, NT, preferred_element_type=F32)
        row_ref[...] = lax.dot_general(rows, perm[...], NT, preferred_element_type=F32)
        for k in range(9):
            count_ref[k] = jnp.sum(jnp.where(block < k, 1.0, 0.0)).astype(jnp.int32)

    sorted_ref[...] = jnp.dot(perm[...], image_ref[...], preferred_element_type=F32).astype(BF16)


def sort_particles(place, slot_class, class_row, pose_row, group_row, defocus_row, images):
    parts, cols = images.shape
    row = pl.BlockSpec((1, parts), lambda i: (0, 0))
    return pl.pallas_call(
        sort_kernel,
        grid=(cols // 512,),
        in_specs=[SMEM, SMEM, row, row, row, row, pl.BlockSpec((parts, 512), lambda i: (0, i))],
        out_specs=[
            pl.BlockSpec((parts, 512), lambda i: (0, i)),
            pl.BlockSpec((parts, parts), lambda i: (0, 0)),
            pl.BlockSpec((parts, 16), lambda i: (0, 0)),
            pl.BlockSpec((16, parts), lambda i: (0, 0)),
            SMEM,
        ],
        out_shape=[
            pltpu.HBM((parts, cols), BF16),
            pltpu.HBM((parts, parts), BF16),
            jax.ShapeDtypeStruct((parts, 16), F32),
            jax.ShapeDtypeStruct((16, parts), F32),
            jax.ShapeDtypeStruct((9,), jnp.int32),
        ],
        scratch_shapes=[pltpu.VMEM((parts, parts), BF16)],
        compiler_params=params(),
        cost_estimate=pl.CostEstimate(
            flops=2 * parts * parts * cols, bytes_accessed=4 * parts * cols, transcendentals=0
        ),
        name="sort_particles",
    )(place, slot_class, class_row, pose_row, group_row, defocus_row, images)


def legendre(q, count):
    x = 2.0 * q - 1.0
    rows = [q * 0.0 + 1.0, x]
    for n in range(1, count - 1):
        rows.append(((2 * n + 1) * x * rows[n] - n * rows[n - 1]) / (n + 1))
    return rows[:count]


def product_rows(freq_x, freq_y):
    q = freq_x * freq_x + freq_y * freq_y
    polys = legendre(q, 5)
    rows = [q * p for p in polys]
    re2, im2 = freq_x * freq_x - freq_y * freq_y, 2.0 * freq_x * freq_y
    re, im = re2, im2
    for count in (5, 4, 3, 2, 1):
        for p in polys[:count]:
            rows += [re * p, im * p]
        re, im = re * re2 - im * im2, re * im2 + im * re2
    return rows


def product_weights():
    angle = np.arange(24) * (2.0 * np.pi / 24) + 0.1
    radius = np.sqrt((np.cos((np.arange(8) + 0.5) * (np.pi / 8)) + 1.0) / 2.0)
    x = (radius[:, None] * np.cos(angle)).reshape(-1)
    y = (radius[:, None] * np.sin(angle)).reshape(-1)
    zern = zernike_rows(x, y)
    pairs = np.stack([zern[j] * zern[k] for j in range(ZERN) for k in range(j, ZERN)], axis=1)
    rows = np.stack(product_rows(x, y), axis=1)
    weights = np.linalg.lstsq(rows, pairs, rcond=None)[0].T
    weights = np.where(np.abs(weights) < 1e-10, 0.0, np.round(weights, 12))
    out = np.zeros((80, RIGHT_AT + 4))
    out[:PAIRS, : rows.shape[1]] = weights
    return out.astype(np.float32)


def pixel_grid(first, count):
    index = first + lax.broadcasted_iota(jnp.int32, (1, count), 1)
    scale = math.sqrt(2.0) / BOX
    freq_x = (index & (BOX // 2 - 1)).astype(F32) * scale
    freq_y = ((index >> 7) - BOX // 2).astype(F32) * scale
    return freq_x, freq_y


def zernike_rows(freq_x, freq_y):
    q = freq_x * freq_x + freq_y * freq_y
    re1, im1 = freq_x, freq_y
    re2 = freq_x * freq_x - freq_y * freq_y
    im2 = 2.0 * freq_x * freq_y
    re3 = re2 * re1 - im2 * im1
    im3 = re2 * im1 + im2 * re1
    re5 = re3 * re2 - im3 * im2
    im5 = re3 * im2 + im3 * re2
    r3 = 3.0 * q - 2.0
    r5 = 10.0 * q * q - 12.0 * q + 3.0
    ro = 5.0 * q - 4.0
    return [re1, im1, r3 * re1, r3 * im1, r5 * re1, r5 * im1, re3, im3, ro * re3, ro * im3, re5, im5]


def tile_edges(stage, parts):
    return [(0, 256, 512, 768), (256, 416, 672, 928, parts), (832, parts)][stage]


def terms_kernel(stage, fill, refs):
    late = stage == 2
    refs = list(refs)
    core = refs.pop(0) if late else None
    first, counts, col_ref, row_ref = refs[:4]
    refs = refs[4:]
    if stage > 0:
        old_moments, old_grads = refs[:2]
        refs = refs[2:]
    image_ref = refs.pop(0)
    refs, work = refs[:-7], refs[-7:]
    table, image, sums, basis, products, table_sem, image_sem = work
    if late:
        keep_ref, send_ref, grad_ref, moment_ref, full = refs[-5:]
        pieces = refs[:-5]
    else:
        moment_ref, grad_ref, token_ref = refs[-3:]
        pieces = refs[:-3]
        token_ref[...] = jnp.zeros_like(token_ref)
    parts = col_ref.shape[0]
    pix_count = image_ref.shape[1] // 2
    kb_from, kb_to = STAGES[stage]
    edges = tile_edges(stage, parts)
    row_from, row_to = edges[0], edges[-1]

    loads = []
    for i, (piece, src, src_col, dst, dst_col, rows, width) in enumerate(fill):
        loads.append(
            pltpu.make_async_copy(
                pieces[piece].at[pl.ds(src, rows), pl.ds(src_col, width)],
                table.at[pl.ds(dst, rows), pl.ds(dst_col, width)],
                table_sem.at[i],
            )
        )
    loads.append(
        pltpu.make_async_copy(image_ref.at[pl.ds(row_from, row_to - row_from), :], image, image_sem.at[0])
    )
    for copy in loads:
        copy.start()
    grad_ref[...] = old_grads[...] if stage > 0 else jnp.zeros_like(grad_ref)
    sums[...] = jnp.zeros_like(sums)
    freq_x, freq_y = pixel_grid(first[0], pix_count)
    q = freq_x * freq_x + freq_y * freq_y

    def lanes(v):
        return sum(v[:, 128 * i : 128 * i + 128] for i in range(v.shape[1] // 128))

    def work_on(at, rows):
        here = slice(at, at + rows)
        there = slice(at - row_from, at - row_from + rows)
        row = (col_ref[here, 0:1] * 256.0 + col_ref[here, 1:2]).astype(jnp.int32) - 256 * kb_from
        col = lax.broadcasted_iota(jnp.int32, (rows, 256 * (kb_to - kb_from)), 1)
        hot = jnp.where(col == row, 1.0, 0.0).astype(BF16)
        defocus = col_ref[here, 2:3] * (PHASE_GAIN / (2.0 * math.pi))
        group_hot = jnp.where(
            lax.broadcasted_iota(jnp.int32, (GROUPS, rows), 0) == row_ref[3:4, here].astype(jnp.int32), 1.0, 0.0
        ).astype(BF16)
        grad_sum = 0.0
        curv_sum = 0.0
        for pix in range(0, pix_count, WIDE):
            cols = slice(pix, pix + WIDE)
            other = slice(pix_count + pix, pix_count + pix + WIDE)
            proj_re = jnp.dot(hot, table[:, cols], preferred_element_type=F32)
            proj_im = jnp.dot(hot, table[:, other], preferred_element_type=F32)
            image_re = image[there, cols].astype(F32)
            image_im = image[there, other].astype(F32)
            q_sub = q[:, cols]

            turns = defocus * q_sub
            rest_turn = turns - jnp.floor(turns + 0.5)
            z = rest_turn * rest_turn
            s = rest_turn * horner(SIN_POLY, z)
            c = horner(COS_POLY, z)
            s2 = s + s
            sin_phi = s2 * c
            cos_phi = 1.0 - s2 * s

            power = proj_re * proj_re + proj_im * proj_im
            along = proj_re * image_re + proj_im * image_im
            across = proj_im * image_re - proj_re * image_im
            weight = (PHASE_GAIN * q_sub) * cos_phi
            sp = sin_phi * power
            grad_sum += lanes(weight * (sp + along))
            curv_sum += lanes(weight * weight * power)
            pred_power = sin_phi * sp
            cross = sin_phi * across

            cross_hi = cross.astype(BF16)
            cross_lo = (cross - cross_hi.astype(F32)).astype(BF16)
            sums[:, cols] += jnp.dot(group_hot, pred_power.astype(BF16), preferred_element_type=F32)
            sums[:, other] += jnp.dot(group_hot, cross_hi, preferred_element_type=F32) + jnp.dot(
                group_hot, cross_lo, preferred_element_type=F32
            )
        grad_ref[0:1, here] += jnp.sum(grad_sum.T, axis=0, keepdims=True)
        grad_ref[1:2, here] += jnp.sum(curv_sum.T, axis=0, keepdims=True)

    products[...] = jnp.zeros_like(products)
    for j, row in enumerate(product_rows(freq_x, freq_y)):
        products[j : j + 1, :] = row
    basis[...] = jnp.zeros_like(basis)
    for j, row in enumerate(zernike_rows(freq_x, freq_y)):
        basis[j : j + 1, :] = row

    for copy in loads:
        copy.wait()
    for at, end in zip(edges[:-1], edges[1:]):
        some = (counts[kb_from] < end) & (counts[kb_to] > at)
        pl.when(some)(functools.partial(work_on, at, end - at))

    normal = lax.dot_general(
        products[...], sums[:, :pix_count], NT, precision=lax.Precision.HIGHEST, preferred_element_type=F32
    )
    right = lax.dot_general(
        basis[...], sums[:, pix_count:], NT, precision=lax.Precision.HIGHEST, preferred_element_type=F32
    )
    moments = jnp.concatenate([normal[:RIGHT_AT], right[:ZERN]], axis=0)
    if stage > 0:
        moments = moments + old_moments[...]
    moment_ref[...] = moments

    if late:
        half = MOMENTS // 2
        full[...] = jnp.zeros_like(full)
        packed = jnp.concatenate([moments[:half], moments[half:]], axis=1)
        full[0:12] = packed[0:12]
        full[16:28] = packed[12:24]
        keep_ref[...] = full[pl.ds(pl.multiple_of(core[0] * 16, 16), 16), :]
        send_ref[...] = full[pl.ds(pl.multiple_of((1 - core[0]) * 16, 16), 16), :]


def particle_terms(stage, fill, first, counts, mark_cols, mark_rows, images, pieces, before=(), core=None):
    parts = mark_cols.shape[0]
    pix_count = images.shape[1] // 2
    late = stage == 2
    operands = [first, counts, mark_cols, mark_rows, *before]
    specs = [SMEM, SMEM] + [VMEM] * (2 + len(before))
    if late:
        operands = [core] + operands
        specs = [SMEM] + specs
    operands += [images, *pieces]
    specs += [pl.BlockSpec(memory_space=pltpu.HBM)] + [pl.BlockSpec(memory_space=pl.ANY)] * len(pieces)
    moments = jax.ShapeDtypeStruct((MOMENTS, GROUPS), F32)
    grads = jax.ShapeDtypeStruct((2, parts), F32)
    half = jax.ShapeDtypeStruct((16, 128), F32)
    kb_from, kb_to = STAGES[stage]
    edges = tile_edges(stage, parts)
    row_from, row_to = edges[0], edges[-1]
    work = [
        pltpu.VMEM((256 * (kb_to - kb_from), 2 * pix_count), BF16),
        pltpu.VMEM((row_to - row_from, 2 * pix_count), BF16),
        pltpu.VMEM((GROUPS, 2 * pix_count), F32),
        pltpu.VMEM((16, pix_count), F32),
        pltpu.VMEM((RIGHT_AT + 4, pix_count), F32),
        pltpu.SemaphoreType.DMA((len(fill),)),
        pltpu.SemaphoreType.DMA((1,)),
    ]
    if late:
        out_shape = [half, half, grads]
        scratch = [pltpu.VMEM(moments.shape, F32), pltpu.VMEM((32, 128), F32)] + work
    else:
        out_shape = [moments, grads, jax.ShapeDtypeStruct((16, pix_count), BF16)]
        scratch = work

    def body(*refs):
        terms_kernel(stage, fill, refs)

    return pl.pallas_call(
        body,
        in_specs=specs,
        out_specs=[VMEM] * len(out_shape),
        out_shape=out_shape,
        scratch_shapes=scratch,
        compiler_params=params(),
        cost_estimate=pl.CostEstimate(
            flops=[4, 3, 1][stage] * 2 * parts * 2048 * pix_count,
            bytes_accessed=8 * 1024 * 1024,
            transcendentals=0,
        ),
        name="terms_%d" % stage,
    )(*operands)


def unsort_kernel(core, grad_ref, perm_ref, keep_ref, send_ref, split, full, perm, perm_sem):
    perm_load = pltpu.make_async_copy(perm_ref, perm, perm_sem.at[0])
    perm_load.start()
    rest = grad_ref[...]
    split[...] = jnp.zeros_like(split)
    for k in range(3):
        term = rest.astype(BF16).astype(F32)
        split[2 * k : 2 * k + 2, :] = term
        rest = rest - term
    perm_load.wait()
    back = jnp.dot(split[...].astype(BF16), perm[...], preferred_element_type=F32)
    grads = back[0:2] + back[2:4] + back[4:6]
    for h in range(2):
        for r in range(4):
            at = 512 * h + 128 * r
            full[8 * h + r : 8 * h + r + 1, :] = grads[0:1, at : at + 128]
            full[8 * h + 4 + r : 8 * h + 5 + r, :] = grads[1:2, at : at + 128]
    keep_ref[...] = full[pl.ds(pl.multiple_of(core[0] * 8, 8), 8), :]
    send_ref[...] = full[pl.ds(pl.multiple_of((1 - core[0]) * 8, 8), 8), :]


def unsort(core, grads, perm):
    half = jax.ShapeDtypeStruct((8, 128), F32)
    return pl.pallas_call(
        unsort_kernel,
        in_specs=[SMEM, VMEM, pl.BlockSpec(memory_space=pltpu.HBM)],
        out_shape=[half, half],
        scratch_shapes=[
            pltpu.VMEM((16, perm.shape[0]), F32),
            pltpu.VMEM((16, 128), F32),
            pltpu.VMEM(perm.shape, BF16),
            pltpu.SemaphoreType.DMA((1,)),
        ],
        compiler_params=params(),
        name="unsort",
    )(core, grads, perm)


def whiten_kernel(core, own_ref, other_ref, weight_ref, white_ref, score_ref, both, rows, sem):
    loads = [
        pltpu.make_async_copy(ref, both.at[pl.ds(pl.multiple_of(at * 24, 8), 24), :], sem.at[i])
        for i, (ref, at) in enumerate([(own_ref, core[0]), (other_ref, 1 - core[0])])
    ]
    for copy in loads:
        copy.start()
    for copy in loads:
        copy.wait()
    low = jnp.concatenate([both[0:12, :], both[24:36, :]], axis=0)
    moments = jnp.concatenate([low[:, :GROUPS], low[:, GROUPS:]], axis=0)
    right = jnp.concatenate([moments[RIGHT_AT:], jnp.zeros((4, GROUPS), F32)], axis=0)
    moments = jnp.dot(
        weight_ref[...], moments[: RIGHT_AT + 4], precision=lax.Precision.HIGHEST, preferred_element_type=F32
    )
    at = 0
    rows[...] = jnp.zeros_like(rows)
    for j in range(ZERN):
        rows[j, j:ZERN, :] = moments[at : at + ZERN - j]
        at += ZERN - j
    line = [rows[j] for j in range(ZERN)]
    lane_row = lax.broadcasted_iota(jnp.int32, (16, GROUPS), 0)
    done = jnp.zeros((16, GROUPS), F32)
    for j in range(ZERN):
        inv = lax.rsqrt(line[j][j : j + 1] + RIDGE)
        col = line[j] * inv
        value = right[j : j + 1] * inv
        done = jnp.where(lane_row == j, value, done)
        right = right - col * value
        for i in range(j + 1, ZERN):
            line[i] = line[i] - col[i : i + 1] * col
    white_ref[...] = done[:ZERN]
    for h in range(2):
        grad = both[24 * h + 16 : 24 * h + 20, :]
        curv = both[24 * h + 20 : 24 * h + 24, :]
        score_ref[4 * h : 4 * h + 4, :] = -grad * lax.rsqrt(curv + 1e-06)


def spread(block, count):
    return jnp.broadcast_to(block[None], (count,) + block.shape)


def reduce_all(core, keep, send, grads, perm):
    mine = keep + lax.ppermute(send, "pix", CORE_SWAP)
    moments = jnp.sum(lax.all_to_all(spread(mine, 8), "dom", 0, 0), axis=0)
    keep, send = unsort(core, grads, perm)
    grads = keep + lax.ppermute(send, "pix", CORE_SWAP)
    mine = jnp.concatenate([moments, grads], axis=0)
    mine = jnp.sum(lax.all_to_all(spread(mine, 16), "pix", 0, 0, axis_index_groups=CORE_GROUPS), axis=0)
    other = lax.ppermute(mine, "pix", CORE_SWAP)
    white, score = pl.pallas_call(
        whiten_kernel,
        in_specs=[SMEM] + [pl.BlockSpec(memory_space=pl.ANY)] * 2 + [VMEM],
        out_shape=[
            jax.ShapeDtypeStruct((ZERN, GROUPS), F32),
            jax.ShapeDtypeStruct((8, 128), F32),
        ],
        scratch_shapes=[
            pltpu.VMEM((48, 128), F32),
            pltpu.VMEM((ZERN, 16, GROUPS), F32),
            pltpu.SemaphoreType.DMA((2,)),
        ],
        compiler_params=params(),
        name="whiten",
    )(core, mine, other, jnp.asarray(product_weights()))
    return white.T, score.reshape(-1)


def hop(block, perm):
    return lax.ppermute(block, "dom", perm)


def fills(pix_count):
    half = pix_count // 2

    def parted(piece, src, dst, rows, at):
        return [(piece, src, part * half, dst, part * pix_count + at, rows, half) for part in range(2)]

    own = [(piece, 0, 0, 256 * piece, 0, 256, 2 * pix_count) for piece in range(4)]
    next_a = parted(0, 0, 0, 256, 0) + parted(1, 0, 256, 256, 0)
    next_b = parted(2, 0, 0, 512, half)
    far = parted(0, 256, 512, 128, 0) + parted(1, 256, 640, 128, 0)
    far += parted(0, 384, 512, 128, half) + parted(1, 384, 640, 128, half)
    last = parted(0, 0, 0, 256, half) + parted(1, 0, 0, 128, 0) + parted(2, 0, 128, 128, 0)
    return [own, next_a + next_b + far, last]


def local(images, slices, class_of, pose_of, group_of, defocus, slot_class):
    parts, _, pix_count = images.shape
    poses = slices.shape[1]
    dom_at = lax.axis_index("dom").astype(jnp.int32).reshape(1)
    pix_at = lax.axis_index("pix").astype(jnp.int32)
    core = (pix_at & 1).reshape(1)
    first = (pix_at * pix_count).reshape(1)
    half = pix_count // 2
    flat = slices.reshape(poses, 2 * pix_count)

    def rows(*blocks):
        return jnp.concatenate(blocks, axis=0)

    def cols(*blocks):
        return jnp.concatenate(blocks, axis=1)

    def part_a(block):
        return cols(block[:, :half], block[:, pix_count : pix_count + half])

    def part_b(block):
        return cols(block[:, half:pix_count], block[:, pix_count + half :])

    side = hop(flat, X_SWAP)
    below = hop(flat, Y_UP)
    above = hop(flat, Y_DOWN)
    image_rows, perm, mark_cols, mark_rows, counts = sort_particles(
        dom_at,
        slot_class,
        class_of.reshape(1, parts),
        pose_of[None, :],
        group_of[None, :],
        defocus.astype(F32)[None, :],
        images.reshape(parts, 2 * pix_count),
    )

    up = hop(rows(part_a(side), part_a(below[:128]), part_b(below[:128]), image_rows[:16, :pix_count]), Y_UP)
    down = hop(rows(part_a(side), part_a(above[128:]), part_b(above[128:])), Y_DOWN)
    b_side = hop(rows(part_b(below), part_b(above)), X_SWAP)
    fill = fills(pix_count)
    shared = (first, counts, mark_cols, mark_rows, image_rows)
    *sums, token = particle_terms(0, fill[0], *shared, [flat, side, below, above])

    far_a_0 = hop(rows(up[:128], token), Y_UP)
    far_a_1 = hop(down[128:256], Y_DOWN)
    far_b = hop(rows(up[384:512], down[384:512]), X_SWAP)
    *sums, _ = particle_terms(1, fill[1], *shared, [up, down, b_side], sums)
    keep, send, grads = particle_terms(2, fill[2], *shared, [far_b, far_a_0, far_a_1], sums, core)
    return reduce_all(core, keep, send, grads, perm)


def solution(mesh):
    return jax.shard_map(
        local,
        mesh=mesh,
        in_specs=(
            P("dom", None, "pix"),
            P("dom", None, None, "pix"),
            P("dom", None),
            P("dom"),
            P("dom"),
            P("dom"),
            P(),
        ),
        out_specs=(P(), P("dom")),
        check_vma=False,
    )
```
